128 devices in a mesh: flop: 8 (over z_hi, x), turn: 16 (over y, z_lo, core).
Axes of the slice: x: 4, y: 4, z: 4 (z_hi: 2, z_lo: 2; z = z_hi * 2 + z_lo), core: 2. Of those that a mesh axis runs over, the one named last changes fastest.
Arguments:
- trunk_regret: float32 [2, 7, 1408], P(None, None, 'turn'), may hold values from 0 to 0.02, as said below
- river_regret: float32 [32, 16, 8, 2, 2, 1408], P('flop', 'turn'), may hold values from 0.01 to 1
- line_pot: float32 [7], replicated, may hold values from 2 to 24
- subgame_line: int32 [32], P('flop'), may hold values from 0 to 6
- alive: int32 [32, 16, 8, 1408], P('flop', 'turn'), may hold values from 0 to 1, as said below
- ranks: int32 [32, 16, 8, 1408], P('flop', 'turn'), may hold values from 0 to 7461
Outputs:
- new_trunk: float32 [2, 7, 1408], P(None, None, 'turn')
- new_river: float32 [32, 16, 8, 2, 2, 1408], P('flop', 'turn')
The draws below stay inside these ranges and needn't reach their ends.
Inputs may be any that keep to these rules, and one draw needn't show every extreme that they name: alive is 1 exactly for hand slots below 1326 whose two cards avoid the board: three flop cards common to a subgame, the turn card common to one turn index of it, and the river card; all these cards are distinct within a subgame. `trunk_regret`: for every player and hand slot some line has a positive regret.
All inputs are finite; a program needn't handle non-finite values.
Results may differ from the reference program's by a relative error of at most 0.0003.
Values sent between devices are 32-bit elements; how exact they have to be, the bound alone decides.
A program may use at most 64 MiB of HBM per device.

```python
import math
import jax
import jax.numpy as jnp
import numpy as np
from jax import lax

CARDS = 52
HPAD = 1408
HANDS = 1326
LINES = 7
RIVERS = 8
SUBGAMES = 32
TURNS = 16


def card_pairs_drawn():
    first_card, second_card = np.triu_indices(CARDS, 1)
    extra = HPAD - first_card.shape[0]
    pad_first = -1 - 2 * np.arange(extra)
    pad_second = -2 - 2 * np.arange(extra)
    return (np.concatenate([first_card, pad_first]).astype(np.int32), np.concatenate([second_card, pad_second]).astype(np.int32))


def draw_alive(key, part):
    key = jax.random.fold_in(key, 11)
    sub_keys = jax.random.split(key, SUBGAMES)
    shuffled = jax.vmap(lambda single: jax.random.permutation(single, CARDS))(sub_keys).astype(jnp.int32)
    flop_cards = shuffled[:, :3]
    turn_cards = shuffled[:, 3:3 + TURNS]
    river_cards = shuffled[:, 3 + TURNS:3 + TURNS + RIVERS]
    first_card, second_card = card_pairs_drawn()
    first_all = jnp.asarray(first_card)
    second_all = jnp.asarray(second_card)

    def card_hits(cards):
        return (cards[..., None] == first_all) | (cards[..., None] == second_all)
    flop_hit = jnp.any(card_hits(flop_cards), axis=1)
    turn_hit = card_hits(turn_cards)
    river_hit = card_hits(river_cards)
    blocked = flop_hit[:, None, None, :] | turn_hit[:, :, None, :] | river_hit[:, None, :, :]
    real_slot = jnp.arange(HPAD) < HANDS
    return jnp.where(blocked | (~real_slot)[None, None, None, :], 0, 1).astype(jnp.int32)


def draw_trunk_regret(key, part):
    key = jax.random.fold_in(key, 23)
    key_size, key_keep, key_line = jax.random.split(key, 3)
    exponent = jax.random.uniform(key_size, (2, LINES, HPAD), jnp.float32, math.log(0.002), math.log(0.02))
    magnitude = jnp.exp(exponent)
    keep_draw = jax.random.uniform(key_keep, (2, LINES, HPAD), jnp.float32)
    chosen = jax.random.randint(key_line, (2, 1, HPAD), 0, LINES).astype(jnp.int32)
    kept = (keep_draw > 0.3) | (jnp.arange(LINES, dtype=jnp.int32)[None, :, None] == chosen)
    return jnp.where(kept, magnitude, 0.0).astype(jnp.float32)


def draw_ranks(key, part):
    key = jax.random.fold_in(key, 29)
    key_strength, key_noise = jax.random.split(key, 2)
    strength = jax.random.randint(key_strength, (SUBGAMES, 1, 1, HPAD), 0, 5000).astype(jnp.int32)
    noise = jax.random.randint(key_noise, (SUBGAMES, TURNS, RIVERS, HPAD), 0, 4000).astype(jnp.int32)
    return jnp.clip(strength + noise - 768, 0, 7461).astype(jnp.int32)


def set_ends(drawn, key, smallest, largest):
    longest = drawn.shape.index(max(drawn.shape))
    spots = []
    for shift in (0, 1):
        where = [jax.random.randint(jax.random.fold_in(key, axis), (), 0, length) for axis, length in enumerate(drawn.shape)]
        where[longest] = (where[longest] + shift) % drawn.shape[longest]
        spots.append(tuple(where))
    return drawn.at[spots[0]].set(smallest).at[spots[1]].set(largest)


def levels(rng, shape, cuts, smallest, largest):
    level = 1.0
    for axis_at, parts in cuts:
        draws = jax.random.uniform(jax.random.fold_in(jax.random.fold_in(rng, 6), axis_at), (parts,), jnp.float32, smallest / len(cuts), largest / len(cuts))
        level = level * jnp.repeat(jnp.exp(draws), shape[axis_at] // parts).reshape((-1,) + (1,) * (len(shape) - 1 - axis_at))
    return level


def setup_inputs(seed: int = 0) -> dict:
    keys = jax.random.split(jax.random.key(seed), 7)
    trunk_regret = draw_trunk_regret(jax.random.fold_in(keys[6], 71), 0)
    river_regret = jnp.clip(jnp.exp(math.log(1.0) - 4.6051702 * jax.random.uniform(keys[1], (SUBGAMES, TURNS, RIVERS, 2, 2, HPAD), jnp.float32) ** levels(keys[1], (SUBGAMES, TURNS, RIVERS, 2, 2, HPAD), ((0, 8), (1, 16)), -0.2, 0.2)), 0.01, 1.0)
    line_pot = jnp.clip(jnp.exp(jax.random.uniform(keys[2], (LINES,), jnp.float32, math.log(2.0), math.log(24.0))), 2.0, 24.0)
    subgame_line = set_ends(jax.random.randint(keys[3], (SUBGAMES,), 0, LINES), jax.random.fold_in(keys[3], 1), 0, LINES - 1).astype(jnp.int32)
    alive = draw_alive(jax.random.fold_in(keys[6], 71), 0)
    ranks = draw_ranks(jax.random.fold_in(keys[6], 71), 0)
    return {"trunk_regret": trunk_regret, "river_regret": river_regret, "line_pot": line_pot, "subgame_line": subgame_line, "alive": alive, "ranks": ranks}


BET_SIZE = 2.0


def card_pairs():
    first_card, second_card = np.triu_indices(CARDS, 1)
    extra = HPAD - first_card.shape[0]
    pad_first = -1 - 2 * np.arange(extra)
    pad_second = -2 - 2 * np.arange(extra)
    return (np.concatenate([first_card, pad_first]).astype(np.int32),
            np.concatenate([second_card, pad_second]).astype(np.int32))


def compat_table():
    first_card, second_card = card_pairs()
    left_one = jnp.asarray(first_card)[:, None]
    left_two = jnp.asarray(second_card)[:, None]
    right_one = jnp.asarray(first_card)[None, :]
    right_two = jnp.asarray(second_card)[None, :]
    collide = (left_one == right_one) | (left_one == right_two) | (left_two == right_one) | (left_two == right_two)
    return jnp.where(collide, 0.0, 1.0).astype(jnp.bfloat16)


def river_inputs(river_regret, reach_probs, live):
    sigma_all = river_regret / jnp.sum(river_regret, axis=4, keepdims=True)
    reach_one = reach_probs[0][:, None, None, :]
    reach_two = reach_probs[1][:, None, None, :]
    two_call = reach_two * sigma_all[:, :, :, 1, 1, :]
    two_fold = reach_two * sigma_all[:, :, :, 1, 0, :]
    one_bet = reach_one * sigma_all[:, :, :, 0, 1, :]
    one_check = reach_one * sigma_all[:, :, :, 0, 0, :]
    reach_wide = jnp.broadcast_to(reach_two, one_bet.shape)
    show_in = (live[:, :, :, None, :] * jnp.stack([reach_wide, two_call, one_bet, one_check], axis=3)).astype(jnp.bfloat16)
    fold_in = (live[:, :, :, None, :] * jnp.stack([two_fold, one_bet], axis=3)).astype(jnp.bfloat16)
    return sigma_all, show_in, fold_in


def river_finish(river_regret, sigma_all, pot_size, live, showdown, fold_sums, norm_count):
    weight = live / norm_count
    half_pot = (0.5 * pot_size)[:, None, None, None]
    call_pot = half_pot + BET_SIZE
    show_val = showdown * weight[:, :, :, None, :]
    fold_val = fold_sums * weight[:, :, :, None, :]
    one_check_val = half_pot * show_val[:, :, :, 0, :]
    one_bet_val = half_pot * fold_val[:, :, :, 0, :] + call_pot * show_val[:, :, :, 1, :]
    two_fold_val = -half_pot * fold_val[:, :, :, 1, :]
    two_call_val = call_pot * show_val[:, :, :, 2, :]
    two_check_line = half_pot * show_val[:, :, :, 3, :]
    one_node = sigma_all[:, :, :, 0, 0, :] * one_check_val + sigma_all[:, :, :, 0, 1, :] * one_bet_val
    two_node = sigma_all[:, :, :, 1, 0, :] * two_fold_val + sigma_all[:, :, :, 1, 1, :] * two_call_val
    one_new = jnp.maximum(river_regret[:, :, :, 0] + jnp.stack([one_check_val, one_bet_val], axis=3) - one_node[:, :, :, None, :], 0.0)
    two_new = jnp.maximum(river_regret[:, :, :, 1] + jnp.stack([two_fold_val, two_call_val], axis=3) - two_node[:, :, :, None, :], 0.0)
    new_river = jnp.stack([one_new, two_new], axis=3)
    root_values = jnp.stack([jnp.sum(one_node, axis=(1, 2)), jnp.sum(two_check_line + two_node, axis=(1, 2))])
    return new_river, root_values


def reference(trunk_regret, river_regret, line_pot, subgame_line, alive, ranks):
    compat = compat_table()
    norm_count = (CARDS - 7) * (CARDS - 8) / 2.0
    sigma_pre = trunk_regret / jnp.sum(trunk_regret, axis=1, keepdims=True)
    onehot = (subgame_line[:, None] == jnp.arange(LINES, dtype=jnp.int32)[None, :]).astype(jnp.float32)
    reach_probs = jnp.einsum("sl,plh->psh", onehot, sigma_pre, precision=lax.Precision.HIGHEST)
    pot_size = jnp.dot(onehot, line_pot, precision=lax.Precision.HIGHEST)
    live = alive.astype(jnp.float32)
    sigma_all, show_in, fold_in = river_inputs(river_regret, reach_probs, live)
    board_count = SUBGAMES * TURNS * RIVERS
    fold_sums = jnp.dot(fold_in.reshape(-1, HPAD), compat, preferred_element_type=jnp.float32).reshape(fold_in.shape)

    def one_board(board_item):
        rank_row, vectors = board_item
        sign_table = jnp.sign(rank_row[None, :] - rank_row[:, None]).astype(jnp.bfloat16) * compat
        return jnp.dot(vectors, sign_table, preferred_element_type=jnp.float32)

    showdown = lax.map(one_board, (ranks.reshape(board_count, HPAD), show_in.reshape(board_count, 4, HPAD)))
    showdown = showdown.reshape(show_in.shape)
    new_river, root_values = river_finish(river_regret, sigma_all, pot_size, live, showdown, fold_sums, norm_count)
    line_values = (LINES / board_count) * jnp.einsum("sl,psh->plh", onehot, root_values, precision=lax.Precision.HIGHEST)
    node_value = jnp.sum(sigma_pre * line_values, axis=1, keepdims=True)
    new_trunk = jnp.maximum(trunk_regret + line_values - node_value, 0.0)
    return new_trunk, new_river
```

```python
import functools

import jax
import jax.numpy as jnp
import numpy as np
from jax import lax
from jax.experimental import pallas as pl
from jax.experimental.pallas import tpu as pltpu
from jax.sharding import PartitionSpec as P

CARDS = 52
BET_SIZE = 2.0
LANES = 128
BLOCK = 256
F32 = jnp.float32
BF16 = jnp.bfloat16
MESH = pl.DeviceIdType.MESH


def card_pairs(slot_count):
    first_card, second_card = np.triu_indices(CARDS, 1)
    extra = slot_count - first_card.shape[0]
    pad_first = -1 - 2 * np.arange(extra)
    pad_second = -2 - 2 * np.arange(extra)
    return (
        np.concatenate([first_card, pad_first]).astype(np.int32),
        np.concatenate([second_card, pad_second]).astype(np.int32),
    )


def compat_table(slot_count):
    first, second = card_pairs(slot_count)
    collide = (
        (first[:, None] == first[None, :])
        | (first[:, None] == second[None, :])
        | (second[:, None] == first[None, :])
        | (second[:, None] == second[None, :])
    )
    return np.where(collide, 0.0, 1.0).astype(np.float32)


def card_table(slot_count):
    first, second = card_pairs(slot_count)
    cards = np.arange(LANES)[None, :]
    return ((first[:, None] == cards) | (second[:, None] == cards)).astype(np.float32)


def roll_lanes(x, shift):
    shift %= x.shape[-1]
    return pltpu.roll(x, shift, 1) if shift else x


def strategy_of(regret):
    return regret / jnp.sum(regret, axis=0, keepdims=True)


def gather_kernel(turns, trunk_ref, out_ref, mine, slots, send_sem, recv_sem):
    flop, turn = lax.axis_index("flop"), lax.axis_index("turn")
    share = trunk_ref.shape[2]
    lines = trunk_ref.shape[1]
    barrier = pltpu.get_barrier_semaphore()
    for step in range(1, turns):
        pl.semaphore_signal(
            barrier, inc=1, device_id=(flop, lax.rem(turn + step, turns)), device_id_type=MESH
        )
    mine[...] = jnp.zeros_like(mine)
    for player in range(2):
        mine[player * 8 : player * 8 + lines, :share] = strategy_of(trunk_ref[player])
    pl.semaphore_wait(barrier, turns - 1)
    copies = []
    for step in range(1, turns):
        copy = pltpu.make_async_remote_copy(
            src_ref=mine,
            dst_ref=slots.at[turn],
            send_sem=send_sem.at[step],
            recv_sem=recv_sem.at[turn],
            device_id=(flop, lax.rem(turn + step, turns)),
            device_id_type=MESH,
        )
        copy.start()
        copies.append(copy)
    slots[turn] = mine[...]
    for step in range(1, turns):
        source = lax.rem(turn + step, turns)
        pltpu.make_async_remote_copy(
            src_ref=mine,
            dst_ref=slots.at[source],
            send_sem=send_sem.at[step],
            recv_sem=recv_sem.at[source],
            device_id=(flop, source),
            device_id_type=MESH,
        ).wait_recv()
    lane = lax.broadcasted_iota(jnp.int32, (16, LANES), 1)
    tiles = [None] * (out_ref.shape[1] // LANES)
    for slot in range(turns):
        tile, offset = divmod(slot * share, LANES)
        piece = roll_lanes(slots[slot], offset)
        low = jnp.where(lane >= offset, piece, 0.0) if offset else piece
        tiles[tile] = low if tiles[tile] is None else tiles[tile] + low
        if offset + share > LANES:
            high = jnp.where(lane < offset + share - LANES, piece, 0.0)
            tiles[tile + 1] = high
    for tile, value in enumerate(tiles):
        out_ref[:, tile * LANES : (tile + 1) * LANES] = value
    for copy in copies:
        copy.wait_send()


def gather_strategies(trunk_regret, turns):
    share = trunk_regret.shape[2]
    return pl.pallas_call(
        functools.partial(gather_kernel, turns),
        out_shape=jax.ShapeDtypeStruct((16, share * turns), F32),
        in_specs=[pl.BlockSpec(memory_space=pltpu.VMEM)],
        out_specs=pl.BlockSpec(memory_space=pltpu.VMEM),
        scratch_shapes=[
            pltpu.VMEM((16, LANES), F32),
            pltpu.VMEM((turns, 16, LANES), F32),
            pltpu.SemaphoreType.DMA((turns,)),
            pltpu.SemaphoreType.DMA((turns,)),
        ],
        compiler_params=pltpu.CompilerParams(collective_id=0, has_side_effects=True),
        name="gather_strategies",
    )(trunk_regret)


def blocks_of(size):
    return [(at, min(BLOCK, size - at)) for at in range(0, size, BLOCK)]


def rank_code(ranks):
    octave = ranks >> 7
    small = (1 << (octave & 15)).astype(F32)
    large = jnp.where(
        octave >= 32,
        jnp.where(octave >= 48, 2.0**48, 2.0**32),
        jnp.where(octave >= 16, 2.0**16, 1.0),
    )
    return ((ranks & 127) + 128).astype(F32) * small * large


def three_parts(x):
    high = x.astype(BF16)
    rest = x - high.astype(F32)
    middle = rest.astype(BF16)
    low = (rest - middle.astype(F32)).astype(BF16)
    return jnp.concatenate([high, middle, low], axis=0)


def load_rows(ref, start, count, stride=1):
    rows = pl.ds(start, count, stride=stride)
    return jnp.concatenate([ref[tile, rows, :] for tile in range(ref.shape[0])], axis=1)


def store_rows(ref, start, count, stride, value):
    rows = pl.ds(start, count, stride=stride)
    for tile in range(ref.shape[0]):
        ref[tile, rows, :] = value[:, tile * LANES : (tile + 1) * LANES]


def stack_rows(rows, count):
    return jnp.broadcast_to(rows[None], (count,) + rows.shape).reshape(
        count * rows.shape[0], rows.shape[1]
    )


def board_kernel(
    hands, line_ref, pot_ref, strategy_ref, regret_ref, alive_ref, ranks_ref, compat_ref, cards_ref, slots_ref,
    out_ref, root_ref, flat, left, sums, code, row_code, column_code,
):
    subgame = pl.program_id(0)
    slots = compat_ref.shape[0]
    rivers = ranks_ref.shape[2]
    line = line_ref[subgame]
    half_pot = 0.5 * pot_ref[line]
    call_pot = half_pot + BET_SIZE
    for river in range(rivers):
        for player in range(2):
            at = river * 4 + player * 2
            store_rows(flat, at, 2, 1, regret_ref[0, 0, river, player])
    code[...] = rank_code(ranks_ref[0, 0])

    def regrets(which):
        return load_rows(flat, which, rivers, 4)

    reach_one = strategy_ref[pl.ds(line, 1), :]
    reach_two = strategy_ref[pl.ds(8 + line, 1), :]
    live = alive_ref[0, 0].astype(F32)
    one_check, one_bet, two_fold, two_call = [regrets(which) for which in range(4)]
    one_sum = one_check + one_bet
    two_sum = two_fold + two_call
    sigma_check, sigma_bet = one_check / one_sum, one_bet / one_sum
    sigma_fold, sigma_call = two_fold / two_sum, two_call / two_sum

    def rounded(x):
        return x.astype(BF16).astype(F32)

    in_bet = rounded(live * (reach_one * sigma_bet))
    in_fold = rounded(live * (reach_two * sigma_fold))
    for row, value in enumerate(
        [
            live * reach_two,
            live * (reach_two * sigma_call),
            in_bet,
            live * (reach_one * sigma_check),
            jnp.zeros_like(live),
            jnp.zeros_like(live),
            jnp.zeros_like(live),
            jnp.zeros_like(live),
        ]
    ):
        store_rows(left, row, rivers, 8, value)

    fold_in = jnp.concatenate([in_fold, in_bet], axis=0)
    per_card = jnp.dot(fold_in.astype(BF16), cards_ref[...], preferred_element_type=F32)
    per_slot = jnp.dot(three_parts(per_card), slots_ref[...], preferred_element_type=F32)
    count = fold_in.shape[0]
    per_slot = per_slot[:count] + per_slot[count : 2 * count] + per_slot[2 * count :]
    fold_sums = jnp.sum(fold_in, axis=1, keepdims=True) - per_slot + fold_in

    def two_boards(pair, carry):
        lefts = []
        for which in range(2):
            river = 2 * pair + which
            one = code[pl.ds(river, 1), :]
            row_code[which] = jnp.broadcast_to(one, (16, slots)).astype(BF16)
            tall = jnp.broadcast_to(one, (LANES, slots)).astype(BF16)
            for at in range(0, slots, LANES):
                column_code[which, at : at + LANES, :] = jnp.transpose(tall[:, at : at + LANES])
            lefts.append(load_rows(left, pl.multiple_of(river * 8, 8), 8).astype(BF16))
        for at, width in blocks_of(slots):
            totals = [None, None]
            for start, depth in blocks_of(hands):
                most = compat_ref[start : start + depth, at : at + width]
                least = -most
                for which in range(2):
                    column = column_code[which, start : start + depth, :]
                    column = jnp.concatenate([column] * (width // LANES), axis=1)
                    row = stack_rows(row_code[which, :, at : at + width], depth // 16)
                    sign = jnp.maximum(jnp.minimum(row - column, most), least)
                    part = jnp.dot(
                        lefts[which][:, start : start + depth], sign, preferred_element_type=F32
                    )
                    totals[which] = part if totals[which] is None else totals[which] + part
            for which in range(2):
                rows = pl.ds(pl.multiple_of((2 * pair + which) * 8, 8), 8)
                for tile in range(width // LANES):
                    sums[at // LANES + tile, rows, :] = totals[which][:, tile * LANES : (tile + 1) * LANES]
        return carry

    lax.fori_loop(0, rivers // 2, two_boards, 0)

    weight = live * (1.0 / ((CARDS - 7) * (CARDS - 8) / 2.0))
    show = [load_rows(sums, row, rivers, 8) * weight for row in range(4)]
    fold_two, fold_one = fold_sums[:rivers] * weight, fold_sums[rivers:] * weight
    check_value = half_pot * show[0]
    bet_value = half_pot * fold_two + call_pot * show[1]
    fold_value = -half_pot * fold_one
    call_value = call_pot * show[2]
    check_line = half_pot * show[3]
    one_node = sigma_check * check_value + sigma_bet * bet_value
    two_node = sigma_fold * fold_value + sigma_call * call_value
    for which, value in enumerate(
        [
            one_check + check_value - one_node,
            one_bet + bet_value - one_node,
            two_fold + fold_value - two_node,
            two_call + call_value - two_node,
        ]
    ):
        store_rows(flat, which, rivers, 4, jnp.maximum(value, 0.0))
    for river in range(rivers):
        for player in range(2):
            at = river * 4 + player * 2
            out_ref[0, 0, river, player] = load_rows(flat, at, 2)
    root_ref[pl.ds(subgame, 1), :] = jnp.sum(one_node, axis=0, keepdims=True)
    root_ref[pl.ds(4 + subgame, 1), :] = jnp.sum(check_line + two_node, axis=0, keepdims=True)


def play_boards(subgame_line, line_pot, strategies, river_regret, alive, ranks):
    subgames, _, rivers, _, _, slots = river_regret.shape
    hands = CARDS * (CARDS - 1) // 2
    hands = -(-hands // 64) * 64
    compat = jnp.asarray(compat_table(slots).astype(jnp.bfloat16))
    cards = jnp.asarray(card_table(slots).astype(jnp.bfloat16))
    card_slots = jnp.asarray(card_table(slots).T.astype(jnp.bfloat16))
    whole = lambda shape: pl.BlockSpec(shape, lambda s: (0,) * len(shape))
    smem = pl.BlockSpec(memory_space=pltpu.SMEM)
    regret_spec = pl.BlockSpec((1, 1, rivers, 2, 2, slots), lambda s: (s, 0, 0, 0, 0, 0))
    slot_spec = pl.BlockSpec((1, 1, rivers, slots), lambda s: (s, 0, 0, 0))
    return pl.pallas_call(
        functools.partial(board_kernel, hands),
        grid=(subgames,),
        out_shape=(
            jax.ShapeDtypeStruct(river_regret.shape, F32),
            jax.ShapeDtypeStruct((2 * subgames, slots), F32),
        ),
        in_specs=[
            smem,
            smem,
            whole(strategies.shape),
            regret_spec,
            slot_spec,
            slot_spec,
            whole(compat.shape),
            whole(cards.shape),
            whole(card_slots.shape),
        ],
        out_specs=(regret_spec, whole((2 * subgames, slots))),
        scratch_shapes=[
            pltpu.VMEM((slots // LANES, 4 * rivers, LANES), F32),
            pltpu.VMEM((slots // LANES, 8 * rivers, LANES), F32),
            pltpu.VMEM((slots // LANES, 8 * rivers, LANES), F32),
            pltpu.VMEM((rivers, slots), F32),
            pltpu.VMEM((2, 16, slots), BF16),
            pltpu.VMEM((2, slots, LANES), BF16),
        ],
        compiler_params=pltpu.CompilerParams(vmem_limit_bytes=40 * 2**20),
        name="play_boards",
    )(subgame_line, line_pot, strategies, river_regret, alive, ranks, compat, cards, card_slots)


def trunk_kernel(
    flops, turns, scale, line_ref, root_ref, trunk_ref, out_ref,
    parts, slots, mine, sums, send_sem, recv_sem, send_sum, recv_sum,
):
    flop, turn = lax.axis_index("flop"), lax.axis_index("turn")
    _, lines, share = trunk_ref.shape
    barrier = pltpu.get_barrier_semaphore()
    for step in range(1, turns):
        pl.semaphore_signal(
            barrier, inc=1, device_id=(flop, lax.rem(turn + step, turns)), device_id_type=MESH
        )
    for step in range(1, flops):
        pl.semaphore_signal(
            barrier, inc=1, device_id=(lax.rem(flop + step, flops), turn), device_id_type=MESH
        )
    lane = lax.broadcasted_iota(jnp.int32, (8, LANES), 1)
    for slot in range(turns):
        tile, offset = divmod(slot * share, LANES)
        piece = roll_lanes(root_ref[:, tile * LANES : (tile + 1) * LANES], -offset)
        if offset + share > LANES:
            after = roll_lanes(root_ref[:, (tile + 1) * LANES : (tile + 2) * LANES], -offset)
            piece = jnp.where(lane < LANES - offset, piece, after)
        parts[slot] = piece
    pl.semaphore_wait(barrier, turns + flops - 2)
    copies = []
    for step in range(1, turns):
        target = lax.rem(turn + step, turns)
        copy = pltpu.make_async_remote_copy(
            src_ref=parts.at[target],
            dst_ref=slots.at[turn],
            send_sem=send_sem.at[step],
            recv_sem=recv_sem.at[turn],
            device_id=(flop, target),
            device_id_type=MESH,
        )
        copy.start()
        copies.append(copy)
    slots[turn] = parts[turn]
    strategies = [strategy_of(trunk_ref[player]) for player in range(2)]
    for step in range(1, turns):
        source = lax.rem(turn + step, turns)
        pltpu.make_async_remote_copy(
            src_ref=parts.at[source],
            dst_ref=slots.at[source],
            send_sem=send_sem.at[step],
            recv_sem=recv_sem.at[source],
            device_id=(flop, source),
            device_id_type=MESH,
        ).wait_recv()
    root = slots[0]
    for slot in range(1, turns):
        root = root + slots[slot]
    subgames = root.shape[0] // 2
    row = lax.broadcasted_iota(jnp.int32, (8, LANES), 0)
    for player in range(2):
        values = jnp.zeros((8, LANES), F32)
        for subgame in range(subgames):
            at = player * subgames + subgame
            values = values + jnp.where(row == line_ref[subgame], root[at : at + 1, :], 0.0)
        mine[player * 8 : player * 8 + 8, :] = values
    for step in range(1, flops):
        copy = pltpu.make_async_remote_copy(
            src_ref=mine,
            dst_ref=sums.at[flop],
            send_sem=send_sum.at[step],
            recv_sem=recv_sum.at[flop],
            device_id=(lax.rem(flop + step, flops), turn),
            device_id_type=MESH,
        )
        copy.start()
        copies.append(copy)
    sums[flop] = mine[...]
    for step in range(1, flops):
        source = lax.rem(flop + step, flops)
        pltpu.make_async_remote_copy(
            src_ref=mine,
            dst_ref=sums.at[source],
            send_sem=send_sum.at[step],
            recv_sem=recv_sum.at[source],
            device_id=(source, turn),
            device_id_type=MESH,
        ).wait_recv()
    total = sums[0]
    for slot in range(1, flops):
        total = total + sums[slot]
    total = total * scale
    for player in range(2):
        values = total[player * 8 : player * 8 + lines, :share]
        node = jnp.sum(strategies[player] * values, axis=0, keepdims=True)
        out_ref[player] = jnp.maximum(trunk_ref[player] + values - node, 0.0)
    for copy in copies:
        copy.wait_send()


def update_trunk(subgame_line, root, trunk_regret, flops, turns, scale):
    return pl.pallas_call(
        functools.partial(trunk_kernel, flops, turns, scale),
        out_shape=jax.ShapeDtypeStruct(trunk_regret.shape, F32),
        in_specs=[
            pl.BlockSpec(memory_space=pltpu.SMEM),
            pl.BlockSpec(memory_space=pltpu.VMEM),
            pl.BlockSpec(memory_space=pltpu.VMEM),
        ],
        out_specs=pl.BlockSpec(memory_space=pltpu.VMEM),
        scratch_shapes=[
            pltpu.VMEM((turns, 8, LANES), F32),
            pltpu.VMEM((turns, 8, LANES), F32),
            pltpu.VMEM((16, LANES), F32),
            pltpu.VMEM((flops, 16, LANES), F32),
            pltpu.SemaphoreType.DMA((turns,)),
            pltpu.SemaphoreType.DMA((turns,)),
            pltpu.SemaphoreType.DMA((flops,)),
            pltpu.SemaphoreType.DMA((flops,)),
        ],
        compiler_params=pltpu.CompilerParams(collective_id=1, has_side_effects=True),
        name="update_trunk",
    )(subgame_line, root, trunk_regret)


def on_device(flops, turns, trunk_regret, river_regret, line_pot, subgame_line, alive, ranks):
    subgames, turn_local, rivers = river_regret.shape[:3]
    boards = subgames * flops * turn_local * turns * rivers
    strategies = gather_strategies(trunk_regret, turns)
    new_river, root = play_boards(subgame_line, line_pot, strategies, river_regret, alive, ranks)
    scale = trunk_regret.shape[1] / boards
    new_trunk = update_trunk(subgame_line, root, trunk_regret, flops, turns, scale)
    return (new_trunk, new_river)


def solution(mesh):
    return jax.shard_map(
        functools.partial(on_device, mesh.shape["flop"], mesh.shape["turn"]),
        mesh=mesh,
        in_specs=(
            P(None, None, "turn"),
            P("flop", "turn", None, None, None, None),
            P(),
            P("flop"),
            P("flop", "turn", None, None),
            P("flop", "turn", None, None),
        ),
        out_specs=(P(None, None, "turn"), P("flop", "turn", None, None, None, None)),
        check_vma=False,
    )
```

```python
import functools

import jax
import jax.numpy as jnp
import numpy as np
from jax import lax
from jax.experimental import pallas as pl
from jax.experimental.pallas import tpu as pltpu
from jax.sharding import PartitionSpec as P

CARDS = 52
BET_SIZE = 2.0
LANES = 128
BLOCK = 256
GROUP = 4
F32 = jnp.float32
BF16 = jnp.bfloat16
MESH = pl.DeviceIdType.MESH


def card_pairs(slot_count, card_count=CARDS):
    first_card, second_card = np.triu_indices(card_count, 1)
    extra = slot_count - first_card.shape[0]
    pad_first = -1 - 2 * np.arange(extra)
    pad_second = -2 - 2 * np.arange(extra)
    return (
        np.concatenate([first_card, pad_first]).astype(np.int32),
        np.concatenate([second_card, pad_second]).astype(np.int32),
    )


def compat_table(slot_count, card_count):
    first, second = card_pairs(slot_count, card_count)
    collide = (
        (first[:, None] == first[None, :])
        | (first[:, None] == second[None, :])
        | (second[:, None] == first[None, :])
        | (second[:, None] == second[None, :])
        | (first[:, None] < 0)
        | (first[None, :] < 0)
    )
    return np.where(collide, 0.0, 1.0).astype(np.float32)


def card_table(slot_count):
    first, second = card_pairs(slot_count)
    cards = np.arange(LANES)[None, :]
    return ((first[:, None] == cards) | (second[:, None] == cards)).astype(np.float32)


def roll_lanes(x, shift):
    shift %= x.shape[-1]
    return pltpu.roll(x, shift, 1) if shift else x


def strategy_of(regret):
    return regret / jnp.sum(regret, axis=0, keepdims=True)


def gather_kernel(turns, trunk_ref, out_ref, mine, slots, send_sem, recv_sem):
    flop, turn = lax.axis_index("flop"), lax.axis_index("turn")
    lines, _, share = trunk_ref.shape
    barrier = pltpu.get_barrier_semaphore()
    for step in range(1, turns):
        pl.semaphore_signal(
            barrier, inc=1, device_id=(flop, lax.rem(turn + step, turns)), device_id_type=MESH
        )
    mine[...] = jnp.zeros_like(mine)
    for player in range(2):
        mine[player * 8 : player * 8 + lines, :share] = strategy_of(trunk_ref[:, player])
    pl.semaphore_wait(barrier, turns - 1)
    copies = []
    for step in range(1, turns):
        copy = pltpu.make_async_remote_copy(
            src_ref=mine,
            dst_ref=slots.at[turn],
            send_sem=send_sem.at[step],
            recv_sem=recv_sem.at[turn],
            device_id=(flop, lax.rem(turn + step, turns)),
            device_id_type=MESH,
        )
        copy.start()
        copies.append(copy)
    slots[turn] = mine[...]
    for step in range(1, turns):
        source = lax.rem(turn + step, turns)
        pltpu.make_async_remote_copy(
            src_ref=mine,
            dst_ref=slots.at[source],
            send_sem=send_sem.at[step],
            recv_sem=recv_sem.at[source],
            device_id=(flop, source),
            device_id_type=MESH,
        ).wait_recv()
    lane = lax.broadcasted_iota(jnp.int32, (16, LANES), 1)
    tiles = [None] * (out_ref.shape[1] // LANES)
    for slot in range(turns):
        tile, offset = divmod(slot * share, LANES)
        piece = roll_lanes(slots[slot], offset)
        low = jnp.where(lane >= offset, piece, 0.0) if offset else piece
        tiles[tile] = low if tiles[tile] is None else tiles[tile] + low
        if offset + share > LANES:
            high = jnp.where(lane < offset + share - LANES, piece, 0.0)
            tiles[tile + 1] = high
    for tile, value in enumerate(tiles):
        out_ref[:, tile * LANES : (tile + 1) * LANES] = value
    for copy in copies:
        copy.wait_send()


def gather_strategies(trunk_regret, turns):
    share = trunk_regret.shape[2]
    return pl.pallas_call(
        functools.partial(gather_kernel, turns),
        out_shape=jax.ShapeDtypeStruct((16, share * turns), F32),
        in_specs=[pl.BlockSpec(memory_space=pltpu.VMEM)],
        out_specs=pl.BlockSpec(memory_space=pltpu.VMEM),
        scratch_shapes=[
            pltpu.VMEM((16, LANES), F32),
            pltpu.VMEM((turns, 16, LANES), F32),
            pltpu.SemaphoreType.DMA((turns,)),
            pltpu.SemaphoreType.DMA((turns,)),
        ],
        compiler_params=pltpu.CompilerParams(collective_id=0, has_side_effects=True),
        name="gather_strategies",
    )(trunk_regret)


def blocks_of(size):
    return [(at, min(BLOCK, size - at)) for at in range(0, size, BLOCK)]


def tiles_of(array):
    return [array[:, at : at + LANES] for at in range(0, array.shape[1], LANES)]


def rank_code(ranks):
    octave = ranks >> 7
    small = (1 << (octave & 15)).astype(F32)
    large = jnp.where(
        octave >= 32,
        jnp.where(octave >= 48, 2.0**48, 2.0**32),
        jnp.where(octave >= 16, 2.0**16, 1.0),
    )
    return ((ranks & 127) + 128).astype(F32) * small * large


def three_parts(x):
    high = x.astype(BF16)
    rest = x - high.astype(F32)
    middle = rest.astype(BF16)
    low = (rest - middle.astype(F32)).astype(BF16)
    return jnp.concatenate([high, middle, low], axis=0)


def load_rows(ref, start, count, stride=1):
    rows = pl.ds(start, count, stride=stride)
    return jnp.concatenate([ref[tile, rows, :] for tile in range(ref.shape[0])], axis=1)


def store_rows(ref, start, count, stride, value):
    rows = pl.ds(start, count, stride=stride)
    for tile, part in enumerate(tiles_of(value)):
        ref[tile, rows, :] = part


def stack_rows(rows, count):
    return jnp.broadcast_to(rows[None], (count,) + rows.shape).reshape(
        count * rows.shape[0], rows.shape[1]
    )


def lanes_at(tiles, tile, source):
    lane = source & (LANES - 1)
    at = source >> 7
    found = None
    for number in tile:
        part = jnp.take_along_axis(tiles[number], lane, axis=1)
        found = part if found is None else jnp.where(at == number, part, found)
    return found


def prefix_counts(marks, ones_ref):
    tiles = tiles_of(marks)
    inner = jnp.dot(jnp.concatenate(tiles, axis=0).astype(BF16), ones_ref[...], preferred_element_type=F32)
    base = jnp.zeros((8, 1), F32)
    counts = []
    for number, tile in enumerate(tiles):
        counts.append(inner[number * 8 : number * 8 + 8] + base)
        base = base + jnp.sum(tile, axis=1, keepdims=True)
    return jnp.concatenate(counts, axis=1).astype(jnp.int32)


def board_kernel(
    line_ref, pot_ref, strategy_ref, regret_hbm, alive_hbm, ranks_hbm, compat_hbm, cards_hbm, slots_hbm, ones_hbm,
    out_hbm, root_ref,
    regret, alive, ranks, compat, cards, card_slots, ones, result, flat, sigma, fold, source, target, left, sums,
    code, row_code, column_code, sems, out_sem,
):
    subgames, _, rivers, _, _, slots = regret.shape
    packed = compat.shape[0]
    copies = [
        pltpu.make_async_copy(hbm, vmem, sems.at[number])
        for number, (hbm, vmem) in enumerate(
            [
                (alive_hbm, alive),
                (ones_hbm, ones),
                (ranks_hbm, ranks),
                (regret_hbm, regret),
                (cards_hbm, cards),
                (slots_hbm, card_slots),
                (compat_hbm, compat),
            ]
        )
    ]
    for copy in copies:
        copy.start()

    copies[0].wait()
    copies[1].wait()
    rows = [jnp.max(alive[s, 0].astype(F32), axis=0, keepdims=True) for s in range(subgames)]
    live_any = jnp.concatenate(rows + [rows[0]] * (8 - subgames), axis=0)
    before = prefix_counts(1.0 - live_any, ones)
    slot = lax.broadcasted_iota(jnp.int32, (8, slots), 1)
    goes = slot - before
    state = jnp.where(live_any > 0.5, before * 2048 + slot, 0)
    for bit in range(8):
        moved = pltpu.roll(state, slots - (1 << bit), 1)
        flag = 2048 << bit
        state = jnp.where(
            (moved & flag) != 0, moved, jnp.where((state & flag) != 0, 0, state)
        )
    comes = state & 2047
    store_rows(target, 0, 8, 1, goes)
    store_rows(source, 0, 8, 1, comes[:, :packed])

    def spread(ref, subgame):
        return [
            jnp.broadcast_to(ref[tile, pl.ds(subgame, 1), :], (8, LANES))
            for tile in range(ref.shape[0])
        ]

    def pack(tiles, sources):
        return jnp.concatenate(
            [lanes_at(tiles, (t, t + 1, t + 2), sources[t]) for t in range(packed // LANES)], axis=1
        )

    def unpack(tiles, targets):
        parts = []
        for t in range(slots // LANES):
            near = [n for n in (t - 2, t - 1, t) if 0 <= n < packed // LANES]
            parts.append(lanes_at(tiles, near, targets[t]))
        return jnp.concatenate(parts, axis=1)

    copies[2].wait()
    copies[3].wait()
    copies[4].wait()
    copies[5].wait()

    def rounded(x):
        return x.astype(BF16).astype(F32)

    def enter(subgame, carry):
        sources = spread(source, subgame)
        first = pl.multiple_of(subgame * rivers, rivers)
        store_rows(code, first, rivers, 1, pack(tiles_of(rank_code(ranks[subgame, 0])), sources))
        base = pl.multiple_of(subgame * 4 * rivers, 4 * rivers)
        for river in range(rivers):
            for player in range(2):
                store_rows(flat, base + river * 4 + player * 2, 2, 1, regret[subgame, 0, river, player])
        line = line_ref[subgame]
        reach_one = strategy_ref[pl.ds(line, 1), :]
        reach_two = strategy_ref[pl.ds(8 + line, 1), :]
        live = alive[subgame, 0].astype(F32)
        one_check, one_bet, two_fold, two_call = [load_rows(flat, base + n, rivers, 4) for n in range(4)]
        one_sum = one_check + one_bet
        two_sum = two_fold + two_call
        parts = [one_check / one_sum, one_bet / one_sum, two_fold / two_sum, two_call / two_sum]
        for number, part in enumerate(parts):
            store_rows(sigma, base + number, rivers, 4, part)
        sigma_check, sigma_bet, sigma_fold, sigma_call = parts
        in_bet = rounded(live * (reach_one * sigma_bet))
        in_fold = rounded(live * (reach_two * sigma_fold))
        shows = [
            live * reach_two,
            live * (reach_two * sigma_call),
            in_bet,
            live * (reach_one * sigma_check),
        ]
        start = pl.multiple_of(subgame * 8 * rivers, 8 * rivers)
        for number, value in enumerate(shows):
            store_rows(left, start + number, rivers, 8, pack(tiles_of(value), sources))
            store_rows(left, start + 4 + number, rivers, 8, jnp.zeros((rivers, packed), F32))
        fold_in = jnp.concatenate([in_fold, in_bet], axis=0)
        per_card = jnp.dot(fold_in.astype(BF16), cards[...], preferred_element_type=F32)
        per_slot = jnp.dot(three_parts(per_card), card_slots[...], preferred_element_type=F32)
        count = fold_in.shape[0]
        per_slot = per_slot[:count] + per_slot[count : 2 * count] + per_slot[2 * count :]
        fold_sums = jnp.sum(fold_in, axis=1, keepdims=True) - per_slot + fold_in
        store_rows(fold, pl.multiple_of(subgame * 2 * rivers, 2 * rivers), 2 * rivers, 1, fold_sums)
        return carry

    lax.fori_loop(0, subgames, enter, 0)
    copies[6].wait()

    def some_boards(group, carry):
        lefts = []
        for which in range(GROUP):
            board = GROUP * group + which
            one = load_rows(code, board, 1)
            row_code[which] = jnp.broadcast_to(one, (16, packed)).astype(BF16)
            tall = jnp.broadcast_to(one, (LANES, packed)).astype(BF16)
            for at in range(0, packed, LANES):
                column_code[which, at : at + LANES, :] = jnp.transpose(tall[:, at : at + LANES])
            lefts.append(load_rows(left, pl.multiple_of(board * 8, 8), 8).astype(BF16))
        for at, width in blocks_of(packed):
            totals = [None] * GROUP
            for start, depth in blocks_of(packed):
                most = compat[start : start + depth, at : at + width]
                least = -most
                for which in range(GROUP):
                    column = column_code[which, start : start + depth, :]
                    column = jnp.concatenate([column] * (width // LANES), axis=1)
                    row = stack_rows(row_code[which, :, at : at + width], depth // 16)
                    sign = jnp.maximum(jnp.minimum(row - column, most), least)
                    part = jnp.dot(
                        lefts[which][:, start : start + depth], sign, preferred_element_type=F32
                    )
                    totals[which] = part if totals[which] is None else totals[which] + part
            for which in range(GROUP):
                rows = pl.ds(pl.multiple_of((GROUP * group + which) * 8, 8), 8)
                for number, part in enumerate(tiles_of(totals[which])):
                    sums[at // LANES + number, rows, :] = part
        return carry

    lax.fori_loop(0, subgames * rivers // GROUP, some_boards, 0)

    def leave(subgame, carry):
        targets = spread(target, subgame)
        base = pl.multiple_of(subgame * 4 * rivers, 4 * rivers)
        start = pl.multiple_of(subgame * 8 * rivers, 8 * rivers)
        half_pot = 0.5 * pot_ref[line_ref[subgame]]
        call_pot = half_pot + BET_SIZE
        live = alive[subgame, 0].astype(F32)
        weight = live * (1.0 / ((CARDS - 7) * (CARDS - 8) / 2.0))
        show = [
            unpack(tiles_of(load_rows(sums, start + number, rivers, 8)), targets) * weight
            for number in range(4)
        ]
        fold_sums = load_rows(fold, pl.multiple_of(subgame * 2 * rivers, 2 * rivers), 2 * rivers)
        fold_two, fold_one = fold_sums[:rivers] * weight, fold_sums[rivers:] * weight
        one_check, one_bet, two_fold, two_call = [load_rows(flat, base + n, rivers, 4) for n in range(4)]
        sigma_check, sigma_bet, sigma_fold, sigma_call = [
            load_rows(sigma, base + n, rivers, 4) for n in range(4)
        ]
        check_value = half_pot * show[0]
        bet_value = half_pot * fold_two + call_pot * show[1]
        fold_value = -half_pot * fold_one
        call_value = call_pot * show[2]
        check_line = half_pot * show[3]
        one_node = sigma_check * check_value + sigma_bet * bet_value
        two_node = sigma_fold * fold_value + sigma_call * call_value
        for number, value in enumerate(
            [
                one_check + check_value - one_node,
                one_bet + bet_value - one_node,
                two_fold + fold_value - two_node,
                two_call + call_value - two_node,
            ]
        ):
            store_rows(flat, base + number, rivers, 4, jnp.maximum(value, 0.0))
        for river in range(rivers):
            for player in range(2):
                result[subgame, 0, river, player] = load_rows(flat, base + river * 4 + player * 2, 2)
        root_ref[pl.ds(subgame, 1), :] = jnp.sum(one_node, axis=0, keepdims=True)
        root_ref[pl.ds(subgames + subgame, 1), :] = jnp.sum(check_line + two_node, axis=0, keepdims=True)
        return carry

    lax.fori_loop(0, subgames, leave, 0)
    copy = pltpu.make_async_copy(result, out_hbm, out_sem)
    copy.start()
    copy.wait()


def play_boards(subgame_line, line_pot, strategies, river_regret, alive, ranks):
    subgames, _, rivers, _, _, slots = river_regret.shape
    packed = -(-((CARDS - 4) * (CARDS - 5) // 2) // LANES) * LANES
    compat = jnp.asarray(compat_table(packed, CARDS - 4).astype(jnp.bfloat16))
    cards = jnp.asarray(card_table(slots).astype(jnp.bfloat16))
    card_slots = jnp.asarray(card_table(slots).T.astype(jnp.bfloat16))
    ones = jnp.asarray(np.triu(np.ones((LANES, LANES)), 1).astype(jnp.bfloat16))
    smem = pl.BlockSpec(memory_space=pltpu.SMEM)
    vmem = pl.BlockSpec(memory_space=pltpu.VMEM)
    hbm = pl.BlockSpec(memory_space=pl.ANY)
    boards = subgames * rivers
    tiles = slots // LANES
    rows = lambda count, tile_count=tiles: pltpu.VMEM((tile_count, count, LANES), F32)
    return pl.pallas_call(
        board_kernel,
        out_shape=(
            jax.ShapeDtypeStruct(river_regret.shape, F32),
            jax.ShapeDtypeStruct((2 * subgames, slots), F32),
        ),
        in_specs=[smem, smem, vmem] + [hbm] * 7,
        out_specs=(hbm, vmem),
        scratch_shapes=[
            pltpu.VMEM(river_regret.shape, F32),
            pltpu.VMEM(alive.shape, jnp.int32),
            pltpu.VMEM(ranks.shape, jnp.int32),
            pltpu.VMEM(compat.shape, BF16),
            pltpu.VMEM(cards.shape, BF16),
            pltpu.VMEM(card_slots.shape, BF16),
            pltpu.VMEM(ones.shape, BF16),
            pltpu.VMEM(river_regret.shape, F32),
            rows(4 * boards),
            rows(4 * boards),
            rows(2 * boards),
            pltpu.VMEM((packed // LANES, 8, LANES), jnp.int32),
            pltpu.VMEM((tiles, 8, LANES), jnp.int32),
            rows(8 * boards, packed // LANES),
            rows(8 * boards, packed // LANES),
            rows(boards, packed // LANES),
            pltpu.VMEM((GROUP, 16, packed), BF16),
            pltpu.VMEM((GROUP, packed, LANES), BF16),
            pltpu.SemaphoreType.DMA((7,)),
            pltpu.SemaphoreType.DMA,
        ],
        compiler_params=pltpu.CompilerParams(vmem_limit_bytes=60 * 2**20),
        name="play_boards",
    )(subgame_line, line_pot, strategies, river_regret, alive, ranks, compat, cards, card_slots, ones)


def trunk_kernel(
    flops, turns, scale, line_ref, root_ref, trunk_ref, out_ref,
    parts, slots, mine, sums, send_sem, recv_sem, send_sum, recv_sum,
):
    flop, turn = lax.axis_index("flop"), lax.axis_index("turn")
    lines, _, share = trunk_ref.shape
    barrier = pltpu.get_barrier_semaphore()
    for step in range(1, turns):
        pl.semaphore_signal(
            barrier, inc=1, device_id=(flop, lax.rem(turn + step, turns)), device_id_type=MESH
        )
    for step in range(1, flops):
        pl.semaphore_signal(
            barrier, inc=1, device_id=(lax.rem(flop + step, flops), turn), device_id_type=MESH
        )
    lane = lax.broadcasted_iota(jnp.int32, (8, LANES), 1)
    for slot in range(turns):
        tile, offset = divmod(slot * share, LANES)
        piece = roll_lanes(root_ref[:, tile * LANES : (tile + 1) * LANES], -offset)
        if offset + share > LANES:
            after = roll_lanes(root_ref[:, (tile + 1) * LANES : (tile + 2) * LANES], -offset)
            piece = jnp.where(lane < LANES - offset, piece, after)
        parts[slot] = piece
    pl.semaphore_wait(barrier, turns + flops - 2)
    copies = []
    for step in range(1, turns):
        target = lax.rem(turn + step, turns)
        copy = pltpu.make_async_remote_copy(
            src_ref=parts.at[target],
            dst_ref=slots.at[turn],
            send_sem=send_sem.at[step],
            recv_sem=recv_sem.at[turn],
            device_id=(flop, target),
            device_id_type=MESH,
        )
        copy.start()
        copies.append(copy)
    slots[turn] = parts[turn]
    strategies = [strategy_of(trunk_ref[:, player]) for player in range(2)]
    for step in range(1, turns):
        source = lax.rem(turn + step, turns)
        pltpu.make_async_remote_copy(
            src_ref=parts.at[source],
            dst_ref=slots.at[source],
            send_sem=send_sem.at[step],
            recv_sem=recv_sem.at[source],
            device_id=(flop, source),
            device_id_type=MESH,
        ).wait_recv()
    root = slots[0]
    for slot in range(1, turns):
        root = root + slots[slot]
    subgames = root.shape[0] // 2
    row = lax.broadcasted_iota(jnp.int32, (8, LANES), 0)
    for player in range(2):
        values = jnp.zeros((8, LANES), F32)
        for subgame in range(subgames):
            at = player * subgames + subgame
            values = values + jnp.where(row == line_ref[subgame], root[at : at + 1, :], 0.0)
        mine[player * 8 : player * 8 + 8, :] = values
    for step in range(1, flops):
        copy = pltpu.make_async_remote_copy(
            src_ref=mine,
            dst_ref=sums.at[flop],
            send_sem=send_sum.at[step],
            recv_sem=recv_sum.at[flop],
            device_id=(lax.rem(flop + step, flops), turn),
            device_id_type=MESH,
        )
        copy.start()
        copies.append(copy)
    sums[flop] = mine[...]
    for step in range(1, flops):
        source = lax.rem(flop + step, flops)
        pltpu.make_async_remote_copy(
            src_ref=mine,
            dst_ref=sums.at[source],
            send_sem=send_sum.at[step],
            recv_sem=recv_sum.at[source],
            device_id=(source, turn),
            device_id_type=MESH,
        ).wait_recv()
    total = sums[0]
    for slot in range(1, flops):
        total = total + sums[slot]
    total = total * scale
    for player in range(2):
        values = total[player * 8 : player * 8 + lines, :share]
        node = jnp.sum(strategies[player] * values, axis=0, keepdims=True)
        out_ref[:, player] = jnp.maximum(trunk_ref[:, player] + values - node, 0.0)
    for copy in copies:
        copy.wait_send()


def update_trunk(subgame_line, root, trunk_regret, flops, turns, scale):
    return pl.pallas_call(
        functools.partial(trunk_kernel, flops, turns, scale),
        out_shape=jax.ShapeDtypeStruct(trunk_regret.shape, F32),
        in_specs=[
            pl.BlockSpec(memory_space=pltpu.SMEM),
            pl.BlockSpec(memory_space=pltpu.VMEM),
            pl.BlockSpec(memory_space=pltpu.VMEM),
        ],
        out_specs=pl.BlockSpec(memory_space=pltpu.VMEM),
        scratch_shapes=[
            pltpu.VMEM((turns, 8, LANES), F32),
            pltpu.VMEM((turns, 8, LANES), F32),
            pltpu.VMEM((16, LANES), F32),
            pltpu.VMEM((flops, 16, LANES), F32),
            pltpu.SemaphoreType.DMA((turns,)),
            pltpu.SemaphoreType.DMA((turns,)),
            pltpu.SemaphoreType.DMA((flops,)),
            pltpu.SemaphoreType.DMA((flops,)),
        ],
        compiler_params=pltpu.CompilerParams(collective_id=1, has_side_effects=True),
        name="update_trunk",
    )(subgame_line, root, trunk_regret)


def on_device(flops, turns, trunk_regret, river_regret, line_pot, subgame_line, alive, ranks):
    subgames, turn_local, rivers = river_regret.shape[:3]
    boards = subgames * flops * turn_local * turns * rivers
    by_line = trunk_regret.transpose(1, 0, 2)
    strategies = gather_strategies(by_line, turns)
    new_river, root = play_boards(subgame_line, line_pot, strategies, river_regret, alive, ranks)
    scale = trunk_regret.shape[1] / boards
    new_trunk = update_trunk(subgame_line, root, by_line, flops, turns, scale)
    return (new_trunk.transpose(1, 0, 2), new_river)


def solution(mesh):
    return jax.shard_map(
        functools.partial(on_device, mesh.shape["flop"], mesh.shape["turn"]),
        mesh=mesh,
        in_specs=(
            P(None, None, "turn"),
            P("flop", "turn", None, None, None, None),
            P(),
            P("flop"),
            P("flop", "turn", None, None),
            P("flop", "turn", None, None),
        ),
        out_specs=(P(None, None, "turn"), P("flop", "turn", None, None, None, None)),
        check_vma=False,
    )
```

```python
import functools

import jax
import jax.numpy as jnp
import numpy as np
from jax import lax
from jax.experimental import pallas as pl
from jax.experimental.pallas import tpu as pltpu
from jax.sharding import PartitionSpec as P

CARDS = 52
BET_SIZE = 2.0
LANES = 128
BLOCK = 256
GROUP = 4
F32 = jnp.float32
BF16 = jnp.bfloat16
MESH = pl.DeviceIdType.MESH


def card_pairs(slot_count, card_count=CARDS):
    first_card, second_card = np.triu_indices(card_count, 1)
    extra = slot_count - first_card.shape[0]
    pad_first = -1 - 2 * np.arange(extra)
    pad_second = -2 - 2 * np.arange(extra)
    return (
        np.concatenate([first_card, pad_first]).astype(np.int32),
        np.concatenate([second_card, pad_second]).astype(np.int32),
    )


def compat_table(slot_count, card_count):
    first, second = card_pairs(slot_count, card_count)
    collide = (
        (first[:, None] == first[None, :])
        | (first[:, None] == second[None, :])
        | (second[:, None] == first[None, :])
        | (second[:, None] == second[None, :])
        | (first[:, None] < 0)
        | (first[None, :] < 0)
    )
    return np.where(collide, 0.0, 1.0).astype(np.float32)


def card_table(slot_count):
    first, second = card_pairs(slot_count)
    cards = np.arange(LANES)[None, :]
    return ((first[:, None] == cards) | (second[:, None] == cards)).astype(np.float32)


def shifted(index, step, size):
    high = lax.rem(lax.div(index, 4) + step // 4, size // 4)
    return high * 4 + lax.rem(lax.rem(index, 4) + step % 4, 4)


def far_first(size, distances):
    high, low = distances
    return sorted(range(1, size), key=lambda step: -(high[step // 4] + low[step % 4]))


def roll_lanes(x, shift):
    shift %= x.shape[-1]
    return pltpu.roll(x, shift, 1) if shift else x


def strategy_of(regret):
    return regret / jnp.sum(regret, axis=0, keepdims=True)


def blocks_of(size):
    return [(at, min(BLOCK, size - at)) for at in range(0, size, BLOCK)]


def tiles_of(array):
    return [array[:, at : at + LANES] for at in range(0, array.shape[1], LANES)]


def rank_code(ranks):
    octave = ranks >> 7
    small = (1 << (octave & 15)).astype(F32)
    large = jnp.where(
        octave >= 32,
        jnp.where(octave >= 48, 2.0**48, 2.0**32),
        jnp.where(octave >= 16, 2.0**16, 1.0),
    )
    return ((ranks & 127) + 128).astype(F32) * small * large


def three_parts(x):
    high = x.astype(BF16)
    rest = x - high.astype(F32)
    middle = rest.astype(BF16)
    low = (rest - middle.astype(F32)).astype(BF16)
    return jnp.concatenate([high, middle, low], axis=0)


def load_rows(ref, start, count, stride=1):
    rows = pl.ds(start, count, stride=stride)
    return jnp.concatenate([ref[tile, rows, :] for tile in range(ref.shape[0])], axis=1)


def store_rows(ref, start, count, stride, value):
    rows = pl.ds(start, count, stride=stride)
    for tile, part in enumerate(tiles_of(value)):
        ref[tile, rows, :] = part


def stack_rows(rows, count):
    return jnp.broadcast_to(rows[None], (count,) + rows.shape).reshape(
        count * rows.shape[0], rows.shape[1]
    )


def lanes_at(tiles, tile, source):
    lane = source & (LANES - 1)
    at = source >> 7
    found = None
    for number in tile:
        part = jnp.take_along_axis(tiles[number], lane, axis=1)
        found = part if found is None else jnp.where(at == number, part, found)
    return found


def prefix_counts(marks, ones_ref):
    tiles = tiles_of(marks)
    inner = jnp.dot(jnp.concatenate(tiles, axis=0).astype(BF16), ones_ref[...], preferred_element_type=F32)
    base = jnp.zeros((8, 1), F32)
    counts = []
    for number, tile in enumerate(tiles):
        counts.append(inner[number * 8 : number * 8 + 8] + base)
        base = base + jnp.sum(tile, axis=1, keepdims=True)
    return jnp.concatenate(counts, axis=1).astype(jnp.int32)


def iteration_kernel(
    flops, turns, scale,
    line_ref, pot_ref, trunk_ref, regret_hbm, alive_hbm, ranks_hbm, compat_hbm, cards_hbm, slots_hbm, ones_hbm,
    trunk_out, river_out,
    regret, alive, ranks, compat, cards, card_slots, ones, flat, sigma, fold, source, target, left, sums,
    code, row_code, column_code, strategy, mine, shares, parts, pieces, values, lines_in,
    sems, out_sem, send_share, recv_share, send_part, recv_part, send_line, recv_line,
):
    flop, turn = lax.axis_index("flop"), lax.axis_index("turn")
    subgames, _, rivers, _, _, slots = regret.shape
    lines, _, share = trunk_ref.shape
    packed = compat.shape[0]

    def turn_peer(step):
        return (flop, shifted(turn, step, turns))

    def flop_peer(step):
        return (shifted(flop, step, flops), turn)

    def remote(src, dst, send, recv, peer):
        return pltpu.make_async_remote_copy(
            src_ref=src, dst_ref=dst, send_sem=send, recv_sem=recv, device_id=peer, device_id_type=MESH
        )

    turn_steps = far_first(turns, ((0, 1, 2, 1), (0, 1, 1, 1)))
    flop_steps = far_first(flops, ((0, 2), (0, 1, 2, 1)))
    copies = [
        pltpu.make_async_copy(hbm, vmem, sems.at[number])
        for number, (hbm, vmem) in enumerate(
            [
                (alive_hbm, alive),
                (ones_hbm, ones),
                (ranks_hbm, ranks),
                (regret_hbm, regret),
                (cards_hbm, cards),
                (slots_hbm, card_slots),
                (compat_hbm, compat),
            ]
        )
    ]
    for copy in copies:
        copy.start()

    barrier = pltpu.get_barrier_semaphore()
    for step in turn_steps:
        pl.semaphore_signal(barrier, inc=1, device_id=turn_peer(step), device_id_type=MESH)
    for step in flop_steps:
        pl.semaphore_signal(barrier, inc=1, device_id=flop_peer(step), device_id_type=MESH)
    mine[...] = jnp.zeros_like(mine)
    own = [strategy_of(trunk_ref[:, player]) for player in range(2)]
    for player in range(2):
        mine[player * 8 : player * 8 + lines, :share] = own[player]
    pl.semaphore_wait(barrier, turns + flops - 2)
    sent = []
    for step in turn_steps:
        sent.append(
            remote(mine, shares.at[turn], send_share.at[step], recv_share.at[turn], turn_peer(step))
        )
        sent[-1].start()
    shares[turn] = mine[...]

    copies[0].wait()
    copies[1].wait()
    rows = [jnp.max(alive[s, 0].astype(F32), axis=0, keepdims=True) for s in range(subgames)]
    live_any = jnp.concatenate(rows + [rows[0]] * (8 - subgames), axis=0)
    before = prefix_counts(1.0 - live_any, ones)
    slot = lax.broadcasted_iota(jnp.int32, (8, slots), 1)
    state = jnp.where(live_any > 0.5, before * 2048 + slot, 0)
    for bit in range(8):
        moved = pltpu.roll(state, slots - (1 << bit), 1)
        flag = 2048 << bit
        state = jnp.where((moved & flag) != 0, moved, jnp.where((state & flag) != 0, 0, state))
    store_rows(target, 0, 8, 1, slot - before)
    store_rows(source, 0, 8, 1, (state & 2047)[:, :packed])

    def spread(ref, subgame):
        return [
            jnp.broadcast_to(ref[tile, pl.ds(subgame, 1), :], (8, LANES))
            for tile in range(ref.shape[0])
        ]

    def pack(tiles, sources):
        return jnp.concatenate(
            [lanes_at(tiles, (t, t + 1, t + 2), sources[t]) for t in range(packed // LANES)], axis=1
        )

    def unpack(tiles, targets):
        found = []
        for t in range(slots // LANES):
            near = [n for n in (t - 2, t - 1, t) if 0 <= n < packed // LANES]
            found.append(lanes_at(tiles, near, targets[t]))
        return jnp.concatenate(found, axis=1)

    for number in range(2, 6):
        copies[number].wait()

    def rounded(x):
        return x.astype(BF16).astype(F32)

    def prepare(subgame, carry):
        sources = spread(source, subgame)
        first = pl.multiple_of(subgame * rivers, rivers)
        store_rows(code, first, rivers, 1, pack(tiles_of(rank_code(ranks[subgame, 0])), sources))
        base = pl.multiple_of(subgame * 4 * rivers, 4 * rivers)
        for river in range(rivers):
            for player in range(2):
                store_rows(flat, base + river * 4 + player * 2, 2, 1, regret[subgame, 0, river, player])
        one_check, one_bet, two_fold, two_call = [load_rows(flat, base + n, rivers, 4) for n in range(4)]
        one_sum = one_check + one_bet
        two_sum = two_fold + two_call
        for number, part in enumerate(
            [one_check / one_sum, one_bet / one_sum, two_fold / two_sum, two_call / two_sum]
        ):
            store_rows(sigma, base + number, rivers, 4, part)
        return carry

    lax.fori_loop(0, subgames, prepare, 0)

    for step in turn_steps:
        peer = turn_peer(step)
        remote(mine, shares.at[peer[1]], send_share.at[step], recv_share.at[peer[1]], peer).wait_recv()
    lane = lax.broadcasted_iota(jnp.int32, (16, LANES), 1)
    tiles = [None] * (slots // LANES)
    for number in range(turns):
        tile, offset = divmod(number * share, LANES)
        piece = roll_lanes(shares[number], offset)
        low = jnp.where(lane >= offset, piece, 0.0) if offset else piece
        tiles[tile] = low if tiles[tile] is None else tiles[tile] + low
        if offset + share > LANES:
            tiles[tile + 1] = jnp.where(lane < offset + share - LANES, piece, 0.0)
    for tile, value in enumerate(tiles):
        strategy[:, tile * LANES : (tile + 1) * LANES] = value

    def enter(subgame, carry):
        sources = spread(source, subgame)
        base = pl.multiple_of(subgame * 4 * rivers, 4 * rivers)
        line = line_ref[subgame]
        reach_one = strategy[pl.ds(line, 1), :]
        reach_two = strategy[pl.ds(8 + line, 1), :]
        live = alive[subgame, 0].astype(F32)
        sigma_check, sigma_bet, sigma_fold, sigma_call = [
            load_rows(sigma, base + n, rivers, 4) for n in range(4)
        ]
        in_bet = rounded(live * (reach_one * sigma_bet))
        in_fold = rounded(live * (reach_two * sigma_fold))
        shows = [
            live * reach_two,
            live * (reach_two * sigma_call),
            in_bet,
            live * (reach_one * sigma_check),
        ]
        start = pl.multiple_of(subgame * 8 * rivers, 8 * rivers)
        for number, value in enumerate(shows):
            store_rows(left, start + number, rivers, 8, pack(tiles_of(value), sources))
            store_rows(left, start + 4 + number, rivers, 8, jnp.zeros((rivers, packed), F32))
        fold_in = jnp.concatenate([in_fold, in_bet], axis=0)
        per_card = jnp.dot(fold_in.astype(BF16), cards[...], preferred_element_type=F32)
        per_slot = jnp.dot(three_parts(per_card), card_slots[...], preferred_element_type=F32)
        count = fold_in.shape[0]
        per_slot = per_slot[:count] + per_slot[count : 2 * count] + per_slot[2 * count :]
        fold_sums = jnp.sum(fold_in, axis=1, keepdims=True) - per_slot + fold_in
        store_rows(fold, pl.multiple_of(subgame * 2 * rivers, 2 * rivers), 2 * rivers, 1, fold_sums)
        return carry

    lax.fori_loop(0, subgames, enter, 0)
    copies[6].wait()

    def some_boards(group, carry):
        lefts = []
        for which in range(GROUP):
            board = GROUP * group + which
            one = load_rows(code, board, 1)
            row_code[which] = jnp.broadcast_to(one, (16, packed)).astype(BF16)
            tall = jnp.broadcast_to(one, (LANES, packed)).astype(BF16)
            for at in range(0, packed, LANES):
                column_code[which, at : at + LANES, :] = jnp.transpose(tall[:, at : at + LANES])
            lefts.append(load_rows(left, pl.multiple_of(board * 8, 8), 8).astype(BF16))
        for at, width in blocks_of(packed):
            totals = [None] * GROUP
            for start, depth in blocks_of(packed):
                most = compat[start : start + depth, at : at + width]
                least = -most
                for which in range(GROUP):
                    column = column_code[which, start : start + depth, :]
                    column = jnp.concatenate([column] * (width // LANES), axis=1)
                    row = stack_rows(row_code[which, :, at : at + width], depth // 16)
                    sign = jnp.maximum(jnp.minimum(row - column, most), least)
                    part = jnp.dot(
                        lefts[which][:, start : start + depth], sign, preferred_element_type=F32
                    )
                    totals[which] = part if totals[which] is None else totals[which] + part
            for which in range(GROUP):
                rows = pl.ds(pl.multiple_of((GROUP * group + which) * 8, 8), 8)
                for number, part in enumerate(tiles_of(totals[which])):
                    sums[at // LANES + number, rows, :] = part
        return carry

    lax.fori_loop(0, subgames * rivers // GROUP, some_boards, 0)

    def leave(subgame, carry):
        targets = spread(target, subgame)
        base = pl.multiple_of(subgame * 4 * rivers, 4 * rivers)
        start = pl.multiple_of(subgame * 8 * rivers, 8 * rivers)
        half_pot = 0.5 * pot_ref[line_ref[subgame]]
        call_pot = half_pot + BET_SIZE
        live = alive[subgame, 0].astype(F32)
        weight = live * (1.0 / ((CARDS - 7) * (CARDS - 8) / 2.0))
        show = [
            unpack(tiles_of(load_rows(sums, start + number, rivers, 8)), targets) * weight
            for number in range(4)
        ]
        fold_sums = load_rows(fold, pl.multiple_of(subgame * 2 * rivers, 2 * rivers), 2 * rivers)
        fold_two, fold_one = fold_sums[:rivers] * weight, fold_sums[rivers:] * weight
        one_check, one_bet, two_fold, two_call = [load_rows(flat, base + n, rivers, 4) for n in range(4)]
        sigma_check, sigma_bet, sigma_fold, sigma_call = [
            load_rows(sigma, base + n, rivers, 4) for n in range(4)
        ]
        check_value = half_pot * show[0]
        bet_value = half_pot * fold_two + call_pot * show[1]
        fold_value = -half_pot * fold_one
        call_value = call_pot * show[2]
        check_line = half_pot * show[3]
        one_node = sigma_check * check_value + sigma_bet * bet_value
        two_node = sigma_fold * fold_value + sigma_call * call_value
        for number, value in enumerate(
            [
                one_check + check_value - one_node,
                one_bet + bet_value - one_node,
                two_fold + fold_value - two_node,
                two_call + call_value - two_node,
            ]
        ):
            store_rows(flat, base + number, rivers, 4, jnp.maximum(value, 0.0))
        roots = [
            jnp.sum(one_node, axis=0, keepdims=True),
            jnp.sum(check_line + two_node, axis=0, keepdims=True),
        ]
        for player in range(2):
            for number, part in enumerate(tiles_of(roots[player])):
                values[number, pl.ds(player * subgames + subgame, 1), :] = part
        return carry

    lax.fori_loop(0, subgames, leave, 0)

    lane = lax.broadcasted_iota(jnp.int32, (8, LANES), 1)
    for number in range(turns):
        tile, offset = divmod(number * share, LANES)
        piece = roll_lanes(values[tile], -offset)
        if offset + share > LANES:
            after = roll_lanes(values[tile + 1], -offset)
            piece = jnp.where(lane < LANES - offset, piece, after)
        parts[number] = piece
    for step in turn_steps:
        peer = turn_peer(step)
        sent.append(
            remote(parts.at[peer[1]], pieces.at[turn], send_part.at[step], recv_part.at[turn], peer)
        )
        sent[-1].start()
    pieces[turn] = parts[turn]

    def write(subgame, carry):
        base = pl.multiple_of(subgame * 4 * rivers, 4 * rivers)
        for river in range(rivers):
            for player in range(2):
                regret[subgame, 0, river, player] = load_rows(flat, base + river * 4 + player * 2, 2)
        return carry

    lax.fori_loop(0, subgames, write, 0)
    out_copy = pltpu.make_async_copy(regret, river_out, out_sem)
    out_copy.start()

    for step in turn_steps:
        peer = turn_peer(step)
        remote(
            parts.at[peer[1]], pieces.at[peer[1]], send_part.at[step], recv_part.at[peer[1]], peer
        ).wait_recv()
    root = pieces[0]
    for number in range(1, turns):
        root = root + pieces[number]
    row = lax.broadcasted_iota(jnp.int32, (8, LANES), 0)
    for player in range(2):
        by_line = jnp.zeros((8, LANES), F32)
        for subgame in range(subgames):
            at = player * subgames + subgame
            by_line = by_line + jnp.where(row == line_ref[subgame], root[at : at + 1, :], 0.0)
        mine_lines = lines_in.at[flop]
        mine_lines[player * 8 : player * 8 + 8, :] = by_line
    for step in flop_steps:
        sent.append(
            remote(
                lines_in.at[flop], lines_in.at[flop], send_line.at[step], recv_line.at[flop], flop_peer(step)
            )
        )
        sent[-1].start()
    for step in flop_steps:
        peer = flop_peer(step)
        remote(
            lines_in.at[flop], lines_in.at[peer[0]], send_line.at[step], recv_line.at[peer[0]], peer
        ).wait_recv()
    total = lines_in[0]
    for number in range(1, flops):
        total = total + lines_in[number]
    total = total * scale
    for player in range(2):
        line_values = total[player * 8 : player * 8 + lines, :share]
        node = jnp.sum(own[player] * line_values, axis=0, keepdims=True)
        trunk_out[:, player] = jnp.maximum(trunk_ref[:, player] + line_values - node, 0.0)
    out_copy.wait()
    for copy in sent:
        copy.wait_send()


def on_device(flops, turns, trunk_regret, river_regret, line_pot, subgame_line, alive, ranks):
    subgames, turn_local, rivers, _, _, slots = river_regret.shape
    lines = trunk_regret.shape[1]
    scale = lines / (subgames * flops * turn_local * turns * rivers)
    packed = -(-((CARDS - 4) * (CARDS - 5) // 2) // LANES) * LANES
    compat = jnp.asarray(compat_table(packed, CARDS - 4).astype(jnp.bfloat16))
    cards = jnp.asarray(card_table(slots).astype(jnp.bfloat16))
    card_slots = jnp.asarray(card_table(slots).T.astype(jnp.bfloat16))
    ones = jnp.asarray(np.triu(np.ones((LANES, LANES)), 1).astype(jnp.bfloat16))
    by_line = trunk_regret.transpose(1, 0, 2)
    smem = pl.BlockSpec(memory_space=pltpu.SMEM)
    vmem = pl.BlockSpec(memory_space=pltpu.VMEM)
    hbm = pl.BlockSpec(memory_space=pl.ANY)
    boards = subgames * rivers
    tiles, packed_tiles = slots // LANES, packed // LANES
    rows = lambda count, tile_count=tiles: pltpu.VMEM((tile_count, count, LANES), F32)
    dma = lambda *shape: pltpu.SemaphoreType.DMA(shape)
    new_trunk, new_river = pl.pallas_call(
        functools.partial(iteration_kernel, flops, turns, scale),
        out_shape=(
            jax.ShapeDtypeStruct(by_line.shape, F32),
            jax.ShapeDtypeStruct(river_regret.shape, F32),
        ),
        in_specs=[smem, smem, vmem] + [hbm] * 7,
        out_specs=(vmem, hbm),
        scratch_shapes=[
            pltpu.VMEM(river_regret.shape, F32),
            pltpu.VMEM(alive.shape, jnp.int32),
            pltpu.VMEM(ranks.shape, jnp.int32),
            pltpu.VMEM(compat.shape, BF16),
            pltpu.VMEM(cards.shape, BF16),
            pltpu.VMEM(card_slots.shape, BF16),
            pltpu.VMEM(ones.shape, BF16),
            rows(4 * boards),
            rows(4 * boards),
            rows(2 * boards),
            pltpu.VMEM((packed_tiles, 8, LANES), jnp.int32),
            pltpu.VMEM((tiles, 8, LANES), jnp.int32),
            rows(8 * boards, packed_tiles),
            rows(8 * boards, packed_tiles),
            rows(boards, packed_tiles),
            pltpu.VMEM((GROUP, 16, packed), BF16),
            pltpu.VMEM((GROUP, packed, LANES), BF16),
            pltpu.VMEM((16, slots), F32),
            pltpu.VMEM((16, LANES), F32),
            rows(16, turns),
            rows(8, turns),
            rows(8, turns),
            rows(8),
            rows(16, flops),
            dma(7),
            pltpu.SemaphoreType.DMA,
            dma(turns),
            dma(turns),
            dma(turns),
            dma(turns),
            dma(flops),
            dma(flops),
        ],
        compiler_params=pltpu.CompilerParams(
            collective_id=0, has_side_effects=True, vmem_limit_bytes=60 * 2**20
        ),
        name="cfr_iteration",
    )(subgame_line, line_pot, by_line, river_regret, alive, ranks, compat, cards, card_slots, ones)
    return (new_trunk.transpose(1, 0, 2), new_river)


def solution(mesh):
    return jax.shard_map(
        functools.partial(on_device, mesh.shape["flop"], mesh.shape["turn"]),
        mesh=mesh,
        in_specs=(
            P(None, None, "turn"),
            P("flop", "turn", None, None, None, None),
            P(),
            P("flop"),
            P("flop", "turn", None, None),
            P("flop", "turn", None, None),
        ),
        out_specs=(P(None, None, "turn"), P("flop", "turn", None, None, None, None)),
        check_vma=False,
    )
```

```python
import functools

import jax
import jax.numpy as jnp
import numpy as np
from jax import lax
from jax.experimental import pallas as pl
from jax.experimental.pallas import tpu as pltpu
from jax.sharding import PartitionSpec as P

CARDS = 52
BET_SIZE = 2.0
LANES = 128
BLOCK = 256
GROUP = 8
F32 = jnp.float32
BF16 = jnp.bfloat16
F8 = jnp.float8_e4m3fn
MESH = pl.DeviceIdType.MESH


def card_pairs(slot_count, card_count=CARDS):
    first_card, second_card = np.triu_indices(card_count, 1)
    extra = slot_count - first_card.shape[0]
    pad_first = -1 - 2 * np.arange(extra)
    pad_second = -2 - 2 * np.arange(extra)
    return (
        np.concatenate([first_card, pad_first]).astype(np.int32),
        np.concatenate([second_card, pad_second]).astype(np.int32),
    )


def compat_table(slot_count, card_count):
    first, second = card_pairs(slot_count, card_count)
    collide = (
        (first[:, None] == first[None, :])
        | (first[:, None] == second[None, :])
        | (second[:, None] == first[None, :])
        | (second[:, None] == second[None, :])
        | (first[:, None] < 0)
        | (first[None, :] < 0)
    )
    return np.where(collide, 0.0, 1.0).astype(np.float32)


def card_table(slot_count):
    first, second = card_pairs(slot_count)
    cards = np.arange(LANES)[None, :]
    return ((first[:, None] == cards) | (second[:, None] == cards)).astype(np.float32)


def shifted(index, step, size):
    high = lax.rem(lax.div(index, 4) + step // 4, size // 4)
    return high * 4 + lax.rem(lax.rem(index, 4) + step % 4, 4)


def far_first(size, distances):
    high, low = distances
    return sorted(range(1, size), key=lambda step: -(high[step // 4] + low[step % 4]))


def roll_lanes(x, shift):
    shift %= x.shape[-1]
    return pltpu.roll(x, shift, 1) if shift else x


def strategy_of(regret):
    return regret / jnp.sum(regret, axis=0, keepdims=True)


def blocks_of(size):
    return [(at, min(BLOCK, size - at)) for at in range(0, size, BLOCK)]


def tiles_of(array):
    return [array[:, at : at + LANES] for at in range(0, array.shape[1], LANES)]


def rank_code(ranks):
    octave = ranks >> 7
    small = (1 << (octave & 15)).astype(F32)
    large = jnp.where(
        octave >= 32,
        jnp.where(octave >= 48, 2.0**48, 2.0**32),
        jnp.where(octave >= 16, 2.0**16, 1.0),
    )
    return ((ranks & 127) + 128).astype(F32) * small * large


def product(rows, table, axis):
    return lax.dot_general(rows, table, (((1,), (axis,)), ((), ())), preferred_element_type=F32)


def three_parts(x):
    high = x.astype(BF16)
    rest = x - high.astype(F32)
    middle = rest.astype(BF16)
    low = (rest - middle.astype(F32)).astype(BF16)
    return jnp.concatenate([high, middle, low], axis=0)


def load_rows(ref, start, count, stride=1):
    rows = pl.ds(start, count, stride=stride)
    return jnp.concatenate([ref[tile, rows, :] for tile in range(ref.shape[0])], axis=1)


def store_rows(ref, start, count, stride, value):
    rows = pl.ds(start, count, stride=stride)
    for tile, part in enumerate(tiles_of(value)):
        ref[tile, rows, :] = part


def stack_rows(rows, count):
    return jnp.broadcast_to(rows[None], (count,) + rows.shape).reshape(
        count * rows.shape[0], rows.shape[1]
    )


def lanes_at(tiles, tile, source):
    lane = source & (LANES - 1)
    at = source >> 7
    found = None
    for number in tile:
        part = jnp.take_along_axis(tiles[number], lane, axis=1)
        found = part if found is None else jnp.where(at == number, part, found)
    return found


def prefix_counts(marks, ones_ref):
    tiles = tiles_of(marks)
    inner = jnp.dot(jnp.concatenate(tiles, axis=0).astype(BF16), ones_ref[...], preferred_element_type=F32)
    base = jnp.zeros((8, 1), F32)
    counts = []
    for number, tile in enumerate(tiles):
        counts.append(inner[number * 8 : number * 8 + 8] + base)
        base = base + jnp.sum(tile, axis=1, keepdims=True)
    return jnp.concatenate(counts, axis=1).astype(jnp.int32)


def iteration_kernel(
    flops, turns, scale,
    line_ref, pot_ref, trunk_ref, regret_hbm, alive_hbm, ranks_hbm, compat_hbm, cards_hbm, slots_hbm, ones_hbm,
    trunk_out, river_out,
    regret, alive, ranks, compat, cards, card_slots, ones, flat, sigma, fold, source, target, left, sums,
    code, row_code, column_code, strategy, mine, shares, parts, pieces, values, lines_in,
    sems, out_sem, send_share, recv_share, send_part, recv_part, send_line, recv_line,
):
    flop, turn = lax.axis_index("flop"), lax.axis_index("turn")
    subgames, _, rivers, _, _, slots = regret.shape
    lines, _, share = trunk_ref.shape
    packed = compat.shape[0]

    def turn_peer(step):
        return (flop, shifted(turn, step, turns))

    def flop_peer(step):
        return (shifted(flop, step, flops), turn)

    def remote(src, dst, send, recv, peer):
        return pltpu.make_async_remote_copy(
            src_ref=src, dst_ref=dst, send_sem=send, recv_sem=recv, device_id=peer, device_id_type=MESH
        )

    turn_steps = far_first(turns, ((0, 1, 2, 1), (0, 1, 1, 1)))
    flop_steps = far_first(flops, ((0, 2), (0, 1, 2, 1)))
    copies = [
        pltpu.make_async_copy(hbm, vmem, sems.at[number])
        for number, (hbm, vmem) in enumerate(
            [
                (alive_hbm, alive),
                (ones_hbm, ones),
                (ranks_hbm, ranks),
                (regret_hbm, regret),
                (cards_hbm, cards),
                (slots_hbm, card_slots),
                (compat_hbm, compat),
            ]
        )
    ]
    for copy in copies:
        copy.start()

    barrier = pltpu.get_barrier_semaphore()
    for step in turn_steps:
        pl.semaphore_signal(barrier, inc=1, device_id=turn_peer(step), device_id_type=MESH)
    for step in flop_steps:
        pl.semaphore_signal(barrier, inc=1, device_id=flop_peer(step), device_id_type=MESH)
    mine[...] = jnp.zeros_like(mine)
    own = [strategy_of(trunk_ref[:, player]) for player in range(2)]
    for player in range(2):
        mine[player * 8 : player * 8 + lines, :share] = own[player]
    pl.semaphore_wait(barrier, turns + flops - 2)
    sent = []
    for step in turn_steps:
        sent.append(
            remote(mine, shares.at[turn], send_share.at[step], recv_share.at[turn], turn_peer(step))
        )
        sent[-1].start()
    shares[turn] = mine[...]

    copies[0].wait()
    copies[1].wait()
    rows = [jnp.max(alive[s, 0].astype(F32), axis=0, keepdims=True) for s in range(subgames)]
    live_any = jnp.concatenate(rows + [rows[0]] * (8 - subgames), axis=0)
    before = prefix_counts(1.0 - live_any, ones)
    slot = lax.broadcasted_iota(jnp.int32, (8, slots), 1)
    state = jnp.where(live_any > 0.5, before * 2048 + slot, 0)
    for bit in range(8):
        moved = pltpu.roll(state, slots - (1 << bit), 1)
        flag = 2048 << bit
        state = jnp.where((moved & flag) != 0, moved, jnp.where((state & flag) != 0, 0, state))
    store_rows(target, 0, 8, 1, slot - before)
    store_rows(source, 0, 8, 1, (state & 2047)[:, :packed])

    def spread(ref, subgame):
        return [
            jnp.broadcast_to(ref[tile, pl.ds(subgame, 1), :], (8, LANES))
            for tile in range(ref.shape[0])
        ]

    def pack(tiles, sources):
        return jnp.concatenate(
            [lanes_at(tiles, (t, t + 1, t + 2), sources[t]) for t in range(packed // LANES)], axis=1
        )

    def unpack(tiles, targets):
        found = []
        for t in range(slots // LANES):
            near = [n for n in (t - 2, t - 1, t) if 0 <= n < packed // LANES]
            found.append(lanes_at(tiles, near, targets[t]))
        return jnp.concatenate(found, axis=1)

    for number in range(2, 6):
        copies[number].wait()

    def rounded(x):
        return x.astype(BF16).astype(F32)

    def prepare(subgame, carry):
        sources = spread(source, subgame)
        first = pl.multiple_of(subgame * rivers, rivers)
        store_rows(code, first, rivers, 1, pack(tiles_of(rank_code(ranks[subgame, 0])), sources))
        base = pl.multiple_of(subgame * 4 * rivers, 4 * rivers)
        for river in range(rivers):
            for player in range(2):
                store_rows(flat, base + river * 4 + player * 2, 2, 1, regret[subgame, 0, river, player])
        one_check, one_bet, two_fold, two_call = [load_rows(flat, base + n, rivers, 4) for n in range(4)]
        one_sum = one_check + one_bet
        two_sum = two_fold + two_call
        for number, part in enumerate(
            [one_check / one_sum, one_bet / one_sum, two_fold / two_sum, two_call / two_sum]
        ):
            store_rows(sigma, base + number, rivers, 4, part)
        return carry

    lax.fori_loop(0, subgames, prepare, 0)

    for step in turn_steps:
        peer = turn_peer(step)
        remote(mine, shares.at[peer[1]], send_share.at[step], recv_share.at[peer[1]], peer).wait_recv()
    lane = lax.broadcasted_iota(jnp.int32, (16, LANES), 1)
    tiles = [None] * (slots // LANES)
    for number in range(turns):
        tile, offset = divmod(number * share, LANES)
        piece = roll_lanes(shares[number], offset)
        low = jnp.where(lane >= offset, piece, 0.0) if offset else piece
        tiles[tile] = low if tiles[tile] is None else tiles[tile] + low
        if offset + share > LANES:
            tiles[tile + 1] = jnp.where(lane < offset + share - LANES, piece, 0.0)
    for tile, value in enumerate(tiles):
        strategy[:, tile * LANES : (tile + 1) * LANES] = value

    def enter(subgame, carry):
        sources = spread(source, subgame)
        base = pl.multiple_of(subgame * 4 * rivers, 4 * rivers)
        line = line_ref[subgame]
        reach_one = strategy[pl.ds(line, 1), :]
        reach_two = strategy[pl.ds(8 + line, 1), :]
        live = alive[subgame, 0].astype(F32)
        sigma_check, sigma_bet, sigma_fold, sigma_call = [
            load_rows(sigma, base + n, rivers, 4) for n in range(4)
        ]
        in_bet = rounded(live * (reach_one * sigma_bet))
        in_fold = rounded(live * (reach_two * sigma_fold))
        shows = [
            live * reach_two,
            live * (reach_two * sigma_call),
            in_bet,
            live * (reach_one * sigma_check),
        ]
        start = pl.multiple_of(subgame * 8 * rivers, 8 * rivers)
        for number, value in enumerate(shows):
            store_rows(left, start + number, rivers, 8, pack(tiles_of(value), sources))
            store_rows(left, start + 4 + number, rivers, 8, jnp.zeros((rivers, packed), F32))
        fold_in = jnp.concatenate([in_fold, in_bet], axis=0)
        per_card = jnp.dot(fold_in.astype(BF16), cards[...], preferred_element_type=F32)
        per_slot = jnp.dot(three_parts(per_card), card_slots[...], preferred_element_type=F32)
        count = fold_in.shape[0]
        per_slot = per_slot[:count] + per_slot[count : 2 * count] + per_slot[2 * count :]
        fold_sums = jnp.sum(fold_in, axis=1, keepdims=True) - per_slot + fold_in
        store_rows(fold, pl.multiple_of(subgame * 2 * rivers, 2 * rivers), 2 * rivers, 1, fold_sums)
        return carry

    lax.fori_loop(0, subgames, enter, 0)
    copies[6].wait()

    def some_boards(group, carry):
        one = jnp.ones((), BF16)
        lefts = []
        for which in range(GROUP):
            board = GROUP * group + which
            codes = load_rows(code, board, 1)
            row_code[which] = jnp.broadcast_to(codes, (16, packed)).astype(BF16)
            tall = jnp.broadcast_to(codes, (LANES, packed)).astype(BF16)
            for at in range(0, packed, LANES):
                column_code[which, at : at + LANES, :] = jnp.transpose(tall[:, at : at + LANES])
            lefts.append(load_rows(left, pl.multiple_of(board * 8, 8), 8).astype(BF16))
        totals = {}

        def add(which, block, part):
            before = totals.get((which, block))
            totals[which, block] = part if before is None else before + part

        blocks = blocks_of(packed)
        for one_side, (start, depth) in enumerate(blocks):
            for other_side, (at, width) in enumerate(blocks):
                if other_side < one_side:
                    continue
                most = compat[start : start + depth, at : at + width]
                for which in range(GROUP):
                    column = column_code[which, start : start + depth, :]
                    column = jnp.concatenate([column] * (width // LANES), axis=1)
                    row = stack_rows(row_code[which, :, at : at + width], depth // 16)
                    sign = jnp.maximum(jnp.minimum(row - column, one), -one) * most
                    sign = sign.astype(F8)
                    part = product(lefts[which][:, start : start + depth], sign, 0)
                    add(which, other_side, part)
                    if other_side > one_side:
                        part = product(lefts[which][:, at : at + width], sign, 1)
                        add(which, one_side, -part)
        for which in range(GROUP):
            rows = pl.ds(pl.multiple_of((GROUP * group + which) * 8, 8), 8)
            for block, (at, _) in enumerate(blocks):
                for number, part in enumerate(tiles_of(totals[which, block])):
                    sums[at // LANES + number, rows, :] = part
        return carry

    lax.fori_loop(0, subgames * rivers // GROUP, some_boards, 0)

    def leave(subgame, carry):
        targets = spread(target, subgame)
        base = pl.multiple_of(subgame * 4 * rivers, 4 * rivers)
        start = pl.multiple_of(subgame * 8 * rivers, 8 * rivers)
        half_pot = 0.5 * pot_ref[line_ref[subgame]]
        call_pot = half_pot + BET_SIZE
        live = alive[subgame, 0].astype(F32)
        weight = live * (1.0 / ((CARDS - 7) * (CARDS - 8) / 2.0))
        show = [
            unpack(tiles_of(load_rows(sums, start + number, rivers, 8)), targets) * weight
            for number in range(4)
        ]
        fold_sums = load_rows(fold, pl.multiple_of(subgame * 2 * rivers, 2 * rivers), 2 * rivers)
        fold_two, fold_one = fold_sums[:rivers] * weight, fold_sums[rivers:] * weight
        one_check, one_bet, two_fold, two_call = [load_rows(flat, base + n, rivers, 4) for n in range(4)]
        sigma_check, sigma_bet, sigma_fold, sigma_call = [
            load_rows(sigma, base + n, rivers, 4) for n in range(4)
        ]
        check_value = half_pot * show[0]
        bet_value = half_pot * fold_two + call_pot * show[1]
        fold_value = -half_pot * fold_one
        call_value = call_pot * show[2]
        check_line = half_pot * show[3]
        one_node = sigma_check * check_value + sigma_bet * bet_value
        two_node = sigma_fold * fold_value + sigma_call * call_value
        for number, value in enumerate(
            [
                one_check + check_value - one_node,
                one_bet + bet_value - one_node,
                two_fold + fold_value - two_node,
                two_call + call_value - two_node,
            ]
        ):
            store_rows(flat, base + number, rivers, 4, jnp.maximum(value, 0.0))
        roots = [
            jnp.sum(one_node, axis=0, keepdims=True),
            jnp.sum(check_line + two_node, axis=0, keepdims=True),
        ]
        for player in range(2):
            for number, part in enumerate(tiles_of(roots[player])):
                values[number, pl.ds(player * subgames + subgame, 1), :] = part
        return carry

    lax.fori_loop(0, subgames, leave, 0)

    lane = lax.broadcasted_iota(jnp.int32, (8, LANES), 1)
    for number in range(turns):
        tile, offset = divmod(number * share, LANES)
        piece = roll_lanes(values[tile], -offset)
        if offset + share > LANES:
            after = roll_lanes(values[tile + 1], -offset)
            piece = jnp.where(lane < LANES - offset, piece, after)
        parts[number] = piece
    for step in turn_steps:
        peer = turn_peer(step)
        sent.append(
            remote(parts.at[peer[1]], pieces.at[turn], send_part.at[step], recv_part.at[turn], peer)
        )
        sent[-1].start()
    pieces[turn] = parts[turn]

    def write(subgame, carry):
        base = pl.multiple_of(subgame * 4 * rivers, 4 * rivers)
        for river in range(rivers):
            for player in range(2):
                regret[subgame, 0, river, player] = load_rows(flat, base + river * 4 + player * 2, 2)
        return carry

    lax.fori_loop(0, subgames, write, 0)
    out_copy = pltpu.make_async_copy(regret, river_out, out_sem)
    out_copy.start()

    for step in turn_steps:
        peer = turn_peer(step)
        remote(
            parts.at[peer[1]], pieces.at[peer[1]], send_part.at[step], recv_part.at[peer[1]], peer
        ).wait_recv()
    root = pieces[0]
    for number in range(1, turns):
        root = root + pieces[number]
    row = lax.broadcasted_iota(jnp.int32, (8, LANES), 0)
    for player in range(2):
        by_line = jnp.zeros((8, LANES), F32)
        for subgame in range(subgames):
            at = player * subgames + subgame
            by_line = by_line + jnp.where(row == line_ref[subgame], root[at : at + 1, :], 0.0)
        mine_lines = lines_in.at[flop]
        mine_lines[player * 8 : player * 8 + 8, :] = by_line
    for step in flop_steps:
        sent.append(
            remote(
                lines_in.at[flop], lines_in.at[flop], send_line.at[step], recv_line.at[flop], flop_peer(step)
            )
        )
        sent[-1].start()
    for step in flop_steps:
        peer = flop_peer(step)
        remote(
            lines_in.at[flop], lines_in.at[peer[0]], send_line.at[step], recv_line.at[peer[0]], peer
        ).wait_recv()
    total = lines_in[0]
    for number in range(1, flops):
        total = total + lines_in[number]
    total = total * scale
    for player in range(2):
        line_values = total[player * 8 : player * 8 + lines, :share]
        node = jnp.sum(own[player] * line_values, axis=0, keepdims=True)
        trunk_out[:, player] = jnp.maximum(trunk_ref[:, player] + line_values - node, 0.0)
    out_copy.wait()
    for copy in sent:
        copy.wait_send()


def on_device(flops, turns, trunk_regret, river_regret, line_pot, subgame_line, alive, ranks):
    subgames, turn_local, rivers, _, _, slots = river_regret.shape
    lines = trunk_regret.shape[1]
    scale = lines / (subgames * flops * turn_local * turns * rivers)
    packed = -(-((CARDS - 4) * (CARDS - 5) // 2) // LANES) * LANES
    compat = jnp.asarray(compat_table(packed, CARDS - 4).astype(jnp.bfloat16))
    cards = jnp.asarray(card_table(slots).astype(jnp.bfloat16))
    card_slots = jnp.asarray(card_table(slots).T.astype(jnp.bfloat16))
    ones = jnp.asarray(np.triu(np.ones((LANES, LANES)), 1).astype(jnp.bfloat16))
    by_line = trunk_regret.transpose(1, 0, 2)
    smem = pl.BlockSpec(memory_space=pltpu.SMEM)
    vmem = pl.BlockSpec(memory_space=pltpu.VMEM)
    hbm = pl.BlockSpec(memory_space=pl.ANY)
    boards = subgames * rivers
    tiles, packed_tiles = slots // LANES, packed // LANES
    rows = lambda count, tile_count=tiles: pltpu.VMEM((tile_count, count, LANES), F32)
    dma = lambda *shape: pltpu.SemaphoreType.DMA(shape)
    new_trunk, new_river = pl.pallas_call(
        functools.partial(iteration_kernel, flops, turns, scale),
        out_shape=(
            jax.ShapeDtypeStruct(by_line.shape, F32),
            jax.ShapeDtypeStruct(river_regret.shape, F32),
        ),
        in_specs=[smem, smem, vmem] + [hbm] * 7,
        out_specs=(vmem, hbm),
        scratch_shapes=[
            pltpu.VMEM(river_regret.shape, F32),
            pltpu.VMEM(alive.shape, jnp.int32),
            pltpu.VMEM(ranks.shape, jnp.int32),
            pltpu.VMEM(compat.shape, BF16),
            pltpu.VMEM(cards.shape, BF16),
            pltpu.VMEM(card_slots.shape, BF16),
            pltpu.VMEM(ones.shape, BF16),
            rows(4 * boards),
            rows(4 * boards),
            rows(2 * boards),
            pltpu.VMEM((packed_tiles, 8, LANES), jnp.int32),
            pltpu.VMEM((tiles, 8, LANES), jnp.int32),
            rows(8 * boards, packed_tiles),
            rows(8 * boards, packed_tiles),
            rows(boards, packed_tiles),
            pltpu.VMEM((GROUP, 16, packed), BF16),
            pltpu.VMEM((GROUP, packed, LANES), BF16),
            pltpu.VMEM((16, slots), F32),
            pltpu.VMEM((16, LANES), F32),
            rows(16, turns),
            rows(8, turns),
            rows(8, turns),
            rows(8),
            rows(16, flops),
            dma(7),
            pltpu.SemaphoreType.DMA,
            dma(turns),
            dma(turns),
            dma(turns),
            dma(turns),
            dma(flops),
            dma(flops),
        ],
        compiler_params=pltpu.CompilerParams(
            collective_id=0, has_side_effects=True, vmem_limit_bytes=60 * 2**20
        ),
        name="cfr_iteration",
    )(subgame_line, line_pot, by_line, river_regret, alive, ranks, compat, cards, card_slots, ones)
    return (new_trunk.transpose(1, 0, 2), new_river)


def solution(mesh):
    return jax.shard_map(
        functools.partial(on_device, mesh.shape["flop"], mesh.shape["turn"]),
        mesh=mesh,
        in_specs=(
            P(None, None, "turn"),
            P("flop", "turn", None, None, None, None),
            P(),
            P("flop"),
            P("flop", "turn", None, None),
            P("flop", "turn", None, None),
        ),
        out_specs=(P(None, None, "turn"), P("flop", "turn", None, None, None, None)),
        check_vma=False,
    )
```

```python
import functools

import jax
import jax.numpy as jnp
import numpy as np
from jax import lax
from jax.experimental import pallas as pl
from jax.experimental.pallas import tpu as pltpu
from jax.sharding import PartitionSpec as P

CARDS = 52
BET_SIZE = 2.0
LANES = 128
BLOCK = 256
READY = 8
FRESH = 6
F32 = jnp.float32
BF16 = jnp.bfloat16
F8 = jnp.float8_e4m3fn
MESH = pl.DeviceIdType.MESH


def card_pairs(slot_count, card_count=CARDS):
    first_card, second_card = np.triu_indices(card_count, 1)
    extra = slot_count - first_card.shape[0]
    pad_first = -1 - 2 * np.arange(extra)
    pad_second = -2 - 2 * np.arange(extra)
    return (
        np.concatenate([first_card, pad_first]).astype(np.int32),
        np.concatenate([second_card, pad_second]).astype(np.int32),
    )


def compat_table(slot_count, card_count):
    first, second = card_pairs(slot_count, card_count)
    collide = (
        (first[:, None] == first[None, :])
        | (first[:, None] == second[None, :])
        | (second[:, None] == first[None, :])
        | (second[:, None] == second[None, :])
        | (first[:, None] < 0)
        | (first[None, :] < 0)
    )
    return np.where(collide, 0.0, 1.0).astype(np.float32)


def card_table(slot_count, card_count):
    first, second = card_pairs(slot_count, card_count)
    cards = np.arange(LANES)[None, :]
    return ((first[:, None] == cards) | (second[:, None] == cards)).astype(np.float32)


def shifted(index, step, size):
    high = lax.rem(lax.div(index, 4) + step // 4, size // 4)
    return high * 4 + lax.rem(lax.rem(index, 4) + step % 4, 4)


def far_first(size, distances):
    high, low = distances
    return sorted(range(1, size), key=lambda step: -(high[step // 4] + low[step % 4]))


def roll_lanes(x, shift):
    shift %= x.shape[-1]
    return pltpu.roll(x, shift, 1) if shift else x


def strategy_of(regret):
    return regret / jnp.sum(regret, axis=0, keepdims=True)


def blocks_of(size):
    return [(at, min(BLOCK, size - at)) for at in range(0, size, BLOCK)]


def tiles_of(array):
    return [array[:, at : at + LANES] for at in range(0, array.shape[1], LANES)]


def rank_code(ranks):
    octave = ranks >> 7
    small = (1 << (octave & 15)).astype(F32)
    large = jnp.where(
        octave >= 32,
        jnp.where(octave >= 48, 2.0**48, 2.0**32),
        jnp.where(octave >= 16, 2.0**16, 1.0),
    )
    return ((ranks & 127) + 128).astype(F32) * small * large


def table_blocks(size):
    sides = blocks_of(size)
    return [
        (start, depth, at, width)
        for number, (start, depth) in enumerate(sides)
        for at, width in sides[number:]
    ]


def product(rows, table, axis):
    return lax.dot_general(rows, table, (((1,), (axis,)), ((), ())), preferred_element_type=F32)


def three_parts(x):
    high = x.astype(BF16)
    rest = x - high.astype(F32)
    middle = rest.astype(BF16)
    low = (rest - middle.astype(F32)).astype(BF16)
    return jnp.concatenate([high, middle, low], axis=0)


def load_rows(ref, start, count, stride=1):
    rows = pl.ds(start, count, stride=stride)
    return jnp.concatenate([ref[tile, rows, :] for tile in range(ref.shape[0])], axis=1)


def store_rows(ref, start, count, stride, value):
    rows = pl.ds(start, count, stride=stride)
    for tile, part in enumerate(tiles_of(value)):
        ref[tile, rows, :] = part


def stack_rows(rows, count):
    return jnp.broadcast_to(rows[None], (count,) + rows.shape).reshape(
        count * rows.shape[0], rows.shape[1]
    )


def lanes_at(tiles, tile, source):
    lane = source & (LANES - 1)
    at = source >> 7
    found = None
    for number in tile:
        part = jnp.take_along_axis(tiles[number], lane, axis=1)
        found = part if found is None else jnp.where(at == number, part, found)
    return found


def prefix_counts(marks, ones_ref):
    tiles = tiles_of(marks)
    inner = jnp.dot(jnp.concatenate(tiles, axis=0).astype(BF16), ones_ref[...], preferred_element_type=F32)
    base = jnp.zeros((8, 1), F32)
    counts = []
    for number, tile in enumerate(tiles):
        counts.append(inner[number * 8 : number * 8 + 8] + base)
        base = base + jnp.sum(tile, axis=1, keepdims=True)
    return jnp.concatenate(counts, axis=1).astype(jnp.int32)


def iteration_kernel(
    flops, turns, scale,
    line_ref, pot_ref, trunk_ref, regret_hbm, alive_hbm, ranks_hbm, compat_hbm, cards_hbm, slots_hbm, ones_hbm,
    trunk_out, river_out,
    regret, alive, ranks, compat, cards, card_slots, ones, flat, sigma, fold, source, target, unblocked, open_slots,
    reach, table, left, sums, code, row_code, column_code, strategy, mine, shares, parts, pieces, values, lines_in,
    sems, out_sem, send_share, recv_share, send_part, recv_part, send_line, recv_line,
):
    flop, turn = lax.axis_index("flop"), lax.axis_index("turn")
    subgames, _, rivers, _, _, slots = regret.shape
    lines, _, share = trunk_ref.shape
    packed = compat.shape[0]
    hands = (CARDS - 4) * (CARDS - 5) // 2

    def turn_peer(step):
        return (flop, shifted(turn, step, turns))

    def flop_peer(step):
        return (shifted(flop, step, flops), turn)

    def remote(src, dst, send, recv, peer):
        return pltpu.make_async_remote_copy(
            src_ref=src, dst_ref=dst, send_sem=send, recv_sem=recv, device_id=peer, device_id_type=MESH
        )

    turn_steps = far_first(turns, ((0, 1, 2, 1), (0, 1, 1, 1)))
    flop_steps = far_first(flops, ((0, 2), (0, 1, 2, 1)))
    copies = [
        pltpu.make_async_copy(hbm, vmem, sems.at[number])
        for number, (hbm, vmem) in enumerate(
            [
                (alive_hbm, alive),
                (ones_hbm, ones),
                (ranks_hbm, ranks),
                (regret_hbm, regret),
                (cards_hbm, cards),
                (slots_hbm, card_slots),
                (compat_hbm, compat),
            ]
        )
    ]
    for copy in copies:
        copy.start()

    barrier = pltpu.get_barrier_semaphore()
    for step in turn_steps:
        pl.semaphore_signal(barrier, inc=1, device_id=turn_peer(step), device_id_type=MESH)
    for step in flop_steps:
        pl.semaphore_signal(barrier, inc=1, device_id=flop_peer(step), device_id_type=MESH)
    mine[...] = jnp.zeros_like(mine)
    own = [strategy_of(trunk_ref[:, player]) for player in range(2)]
    for player in range(2):
        mine[player * 8 : player * 8 + lines, :share] = own[player]
    pl.semaphore_wait(barrier, turns + flops - 2)
    sent = []
    for step in turn_steps:
        sent.append(
            remote(mine, shares.at[turn], send_share.at[step], recv_share.at[turn], turn_peer(step))
        )
        sent[-1].start()
    shares[turn] = mine[...]

    copies[0].wait()
    copies[1].wait()
    rows = [jnp.max(alive[s, 0].astype(F32), axis=0, keepdims=True) for s in range(subgames)]
    live_any = jnp.concatenate(rows + rows, axis=0)
    before = prefix_counts(1.0 - live_any, ones)
    slot = lax.broadcasted_iota(jnp.int32, (8, slots), 1)
    state = jnp.where(live_any > 0.5, before * 2048 + slot, 0)
    for bit in range(8):
        moved = pltpu.roll(state, slots - (1 << bit), 1)
        flag = 2048 << bit
        state = jnp.where((moved & flag) != 0, moved, jnp.where((state & flag) != 0, 0, state))
    store_rows(target, 0, 8, 1, slot - before)
    store_rows(unblocked, 0, 8, 1, live_any)
    store_rows(source, 0, 8, 1, (state & 2047)[:, :packed])

    def spread(ref, subgame):
        return [
            jnp.broadcast_to(ref[tile, pl.ds(subgame, 1), :], (8, LANES))
            for tile in range(ref.shape[0])
        ]

    def pack(tiles, sources):
        return jnp.concatenate(
            [lanes_at(tiles, (t, t + 1, t + 2), sources[t]) for t in range(packed // LANES)], axis=1
        )

    def unpack(tiles, targets):
        found = []
        for t in range(slots // LANES):
            near = [n for n in (t - 2, t - 1, t) if 0 <= n < packed // LANES]
            found.append(lanes_at(tiles, near, targets[t]))
        return jnp.concatenate(found, axis=1)

    for number in range(2, 6):
        copies[number].wait()

    def rounded(x):
        return x.astype(BF16).astype(F32)

    def prepare(subgame, carry):
        sources = spread(source, subgame)
        first = pl.multiple_of(subgame * rivers, rivers)
        base = pl.multiple_of(subgame * 4 * rivers, 4 * rivers)
        store_rows(code, first, rivers, 1, pack(tiles_of(rank_code(ranks[subgame, 0])), sources))
        for river in range(rivers):
            for player in range(2):
                store_rows(flat, base + river * 4 + player * 2, 2, 1, regret[subgame, 0, river, player])
        one_check, one_bet, two_fold, two_call = [
            pack(tiles_of(load_rows(flat, base + n, rivers, 4)), sources) for n in range(4)
        ]
        one_sum = one_check + one_bet
        two_sum = two_fold + two_call
        for number, part in enumerate(
            [one_check / one_sum, one_bet / one_sum, two_fold / two_sum, two_call / two_sum]
        ):
            store_rows(sigma, base + number, rivers, 4, part)
        at = lax.broadcasted_iota(jnp.int32, (rivers, packed), 1)
        live = pack(tiles_of(alive[subgame, 0].astype(F32)), sources)
        store_rows(open_slots, first, rivers, 1, jnp.where(at < hands, live, 0.0))
        return carry

    lax.fori_loop(0, subgames, prepare, 0)
    copies[6].wait()

    blocks = table_blocks(packed)

    def ready_codes(first, count):
        for which in range(count):
            codes = load_rows(code, first + which, 1)
            row_code[which] = jnp.broadcast_to(codes, (16, packed)).astype(BF16)
            tall = jnp.broadcast_to(codes, (LANES, packed)).astype(BF16)
            for at in range(0, packed, LANES):
                column_code[which, at : at + LANES, :] = jnp.transpose(tall[:, at : at + LANES])

    def sign_block(which, block, most):
        start, depth, at, width = block
        one = jnp.ones((), BF16)
        column = column_code[which, start : start + depth, :]
        column = jnp.concatenate([column] * (width // LANES), axis=1)
        row = stack_rows(row_code[which, :, at : at + width], depth // 16)
        return (jnp.maximum(jnp.minimum(row - column, one), -one) * most).astype(F8)

    def masks(block):
        start, depth, at, width = block
        return compat[start : start + depth, at : at + width]

    def play(boards, sign_of):
        lefts = [load_rows(left, pl.multiple_of(board * 8, 8), 8).astype(BF16) for board in boards]
        totals = {}

        def add(which, at, part):
            for number, piece in enumerate(tiles_of(part)):
                key = (which, at // LANES + number)
                totals[key] = totals[key] + piece if key in totals else piece

        for block in blocks:
            start, depth, at, width = block
            most = masks(block)
            for which in range(len(boards)):
                sign = sign_of(which, block, most)
                add(which, at, product(lefts[which][:, start : start + depth], sign, 0))
                if at > start:
                    add(which, start, -product(lefts[which][:, at : at + width], sign, 1))
        for which, board in enumerate(boards):
            rows = pl.ds(pl.multiple_of(board * 8, 8), 8)
            for number in range(packed // LANES):
                sums[number, rows, :] = totals[which, number]

    def tables(block):
        start, depth, at, width = block
        return [(slice(start, start + depth), at // LANES + n) for n in range(width // LANES)]

    def build_first():
        ready_codes(0, READY)
        for block in blocks:
            most = masks(block)
            for which in range(READY):
                for (rows, tile), part in zip(tables(block), tiles_of(sign_block(which, block, most))):
                    table[which, tile, rows, :] = part

    def built(which, block):
        return jnp.concatenate([table[which, tile, rows, :] for rows, tile in tables(block)], axis=1)

    steps = (subgames * rivers - READY) // FRESH
    ready = READY // steps

    def some_boards(step, carry):
        first = READY + step * FRESH
        ready_codes(first, FRESH)

        def sign_of(which, block, most):
            if which < FRESH:
                return sign_block(which, block, most)
            return built(step * ready + which - FRESH, block)

        play([first + n for n in range(FRESH)] + [step * ready + n for n in range(ready)], sign_of)
        return carry

    build_first()

    for step in turn_steps:
        peer = turn_peer(step)
        remote(mine, shares.at[peer[1]], send_share.at[step], recv_share.at[peer[1]], peer).wait_recv()
    lane = lax.broadcasted_iota(jnp.int32, (16, LANES), 1)
    tiles = [None] * (slots // LANES)
    for number in range(turns):
        tile, offset = divmod(number * share, LANES)
        piece = roll_lanes(shares[number], offset)
        low = jnp.where(lane >= offset, piece, 0.0) if offset else piece
        tiles[tile] = low if tiles[tile] is None else tiles[tile] + low
        if offset + share > LANES:
            tiles[tile + 1] = jnp.where(lane < offset + share - LANES, piece, 0.0)
    for tile, value in enumerate(tiles):
        strategy[:, tile * LANES : (tile + 1) * LANES] = value
    chosen = [
        strategy[pl.ds(8 * player + line_ref[subgame], 1), :]
        for player in range(2)
        for subgame in range(subgames)
    ]
    chosen = tiles_of(jnp.concatenate(chosen, axis=0))
    store_rows(reach, 0, 8, 1, pack(chosen, [source[t] for t in range(packed // LANES)]))

    def enter(subgame, carry):
        first = pl.multiple_of(subgame * rivers, rivers)
        base = pl.multiple_of(subgame * 4 * rivers, 4 * rivers)
        reach_one = load_rows(reach, subgame, 1)
        reach_two = load_rows(reach, subgames + subgame, 1)
        live = load_rows(open_slots, first, rivers)
        sigma_check, sigma_bet, sigma_fold, sigma_call = [
            load_rows(sigma, base + n, rivers, 4) for n in range(4)
        ]
        in_bet = rounded(live * (reach_one * sigma_bet))
        in_fold = rounded(live * (reach_two * sigma_fold))
        shows = [
            live * reach_two,
            live * (reach_two * sigma_call),
            in_bet,
            live * (reach_one * sigma_check),
        ]
        start = pl.multiple_of(subgame * 8 * rivers, 8 * rivers)
        for number, value in enumerate(shows):
            store_rows(left, start + number, rivers, 8, value)
            store_rows(left, start + 4 + number, rivers, 8, jnp.zeros((rivers, packed), F32))
        fold_in = jnp.concatenate([in_fold, in_bet], axis=0)
        per_card = jnp.dot(fold_in.astype(BF16), cards[...], preferred_element_type=F32)
        per_slot = jnp.dot(three_parts(per_card), card_slots[...], preferred_element_type=F32)
        count = fold_in.shape[0]
        per_slot = per_slot[:count] + per_slot[count : 2 * count] + per_slot[2 * count :]
        fold_sums = jnp.sum(fold_in, axis=1, keepdims=True) - per_slot + fold_in
        store_rows(fold, pl.multiple_of(subgame * 2 * rivers, 2 * rivers), 2 * rivers, 1, fold_sums)
        return carry

    lax.fori_loop(0, subgames, enter, 0)

    lax.fori_loop(0, steps, some_boards, 0)

    def leave(subgame, carry):
        first = pl.multiple_of(subgame * rivers, rivers)
        base = pl.multiple_of(subgame * 4 * rivers, 4 * rivers)
        start = pl.multiple_of(subgame * 8 * rivers, 8 * rivers)
        half_pot = 0.5 * pot_ref[line_ref[subgame]]
        call_pot = half_pot + BET_SIZE
        live = load_rows(open_slots, first, rivers)
        weight = live * (1.0 / ((CARDS - 7) * (CARDS - 8) / 2.0))
        show = [load_rows(sums, start + number, rivers, 8) * weight for number in range(4)]
        fold_sums = load_rows(fold, pl.multiple_of(subgame * 2 * rivers, 2 * rivers), 2 * rivers)
        fold_two, fold_one = fold_sums[:rivers] * weight, fold_sums[rivers:] * weight
        sigma_check, sigma_bet, sigma_fold, sigma_call = [
            load_rows(sigma, base + n, rivers, 4) for n in range(4)
        ]
        check_value = half_pot * show[0]
        bet_value = half_pot * fold_two + call_pot * show[1]
        fold_value = -half_pot * fold_one
        call_value = call_pot * show[2]
        check_line = half_pot * show[3]
        one_node = sigma_check * check_value + sigma_bet * bet_value
        two_node = sigma_fold * fold_value + sigma_call * call_value
        for number, value in enumerate(
            [check_value - one_node, bet_value - one_node, fold_value - two_node, call_value - two_node]
        ):
            store_rows(sigma, base + number, rivers, 4, value)
        roots = [
            jnp.sum(one_node, axis=0, keepdims=True),
            jnp.sum(check_line + two_node, axis=0, keepdims=True),
        ]
        for player in range(2):
            store_rows(values, player * subgames + subgame, 1, 1, roots[player])
        return carry

    lax.fori_loop(0, subgames, leave, 0)

    lane = lax.broadcasted_iota(jnp.int32, (8, LANES), 1)
    roots = [values[t] for t in range(packed // LANES)]
    roots = tiles_of(unpack(roots, [target[t] for t in range(slots // LANES)]))
    roots = [part * unblocked[t] for t, part in enumerate(roots)]
    for number in range(turns):
        tile, offset = divmod(number * share, LANES)
        piece = roll_lanes(roots[tile], -offset)
        if offset + share > LANES:
            after = roll_lanes(roots[tile + 1], -offset)
            piece = jnp.where(lane < LANES - offset, piece, after)
        parts[number] = piece
    for step in turn_steps:
        peer = turn_peer(step)
        sent.append(
            remote(parts.at[peer[1]], pieces.at[turn], send_part.at[step], recv_part.at[turn], peer)
        )
        sent[-1].start()
    pieces[turn] = parts[turn]

    def write(subgame, carry):
        targets = spread(target, subgame)
        base = pl.multiple_of(subgame * 4 * rivers, 4 * rivers)
        live = alive[subgame, 0].astype(F32)
        for number in range(4):
            change = unpack(tiles_of(load_rows(sigma, base + number, rivers, 4)), targets) * live
            value = jnp.maximum(load_rows(flat, base + number, rivers, 4) + change, 0.0)
            store_rows(flat, base + number, rivers, 4, value)
        for river in range(rivers):
            for player in range(2):
                regret[subgame, 0, river, player] = load_rows(flat, base + river * 4 + player * 2, 2)
        return carry

    lax.fori_loop(0, subgames, write, 0)
    out_copy = pltpu.make_async_copy(regret, river_out, out_sem)
    out_copy.start()

    for step in turn_steps:
        peer = turn_peer(step)
        remote(
            parts.at[peer[1]], pieces.at[peer[1]], send_part.at[step], recv_part.at[peer[1]], peer
        ).wait_recv()
    root = pieces[0]
    for number in range(1, turns):
        root = root + pieces[number]
    row = lax.broadcasted_iota(jnp.int32, (8, LANES), 0)
    for player in range(2):
        by_line = jnp.zeros((8, LANES), F32)
        for subgame in range(subgames):
            at = player * subgames + subgame
            by_line = by_line + jnp.where(row == line_ref[subgame], root[at : at + 1, :], 0.0)
        mine_lines = lines_in.at[flop]
        mine_lines[player * 8 : player * 8 + 8, :] = by_line
    for step in flop_steps:
        sent.append(
            remote(
                lines_in.at[flop], lines_in.at[flop], send_line.at[step], recv_line.at[flop], flop_peer(step)
            )
        )
        sent[-1].start()
    for step in flop_steps:
        peer = flop_peer(step)
        remote(
            lines_in.at[flop], lines_in.at[peer[0]], send_line.at[step], recv_line.at[peer[0]], peer
        ).wait_recv()
    total = lines_in[0]
    for number in range(1, flops):
        total = total + lines_in[number]
    total = total * scale
    for player in range(2):
        line_values = total[player * 8 : player * 8 + lines, :share]
        node = jnp.sum(own[player] * line_values, axis=0, keepdims=True)
        trunk_out[:, player] = jnp.maximum(trunk_ref[:, player] + line_values - node, 0.0)
    out_copy.wait()
    for copy in sent:
        copy.wait_send()


def on_device(flops, turns, trunk_regret, river_regret, line_pot, subgame_line, alive, ranks):
    subgames, turn_local, rivers, _, _, slots = river_regret.shape
    lines = trunk_regret.shape[1]
    scale = lines / (subgames * flops * turn_local * turns * rivers)
    packed = -(-((CARDS - 4) * (CARDS - 5) // 2) // LANES) * LANES
    compat = jnp.asarray(compat_table(packed, CARDS - 4).astype(jnp.bfloat16))
    cards = jnp.asarray(card_table(packed, CARDS - 4).astype(jnp.bfloat16))
    card_slots = jnp.asarray(card_table(packed, CARDS - 4).T.astype(jnp.bfloat16))
    ones = jnp.asarray(np.triu(np.ones((LANES, LANES)), 1).astype(jnp.bfloat16))
    by_line = trunk_regret.transpose(1, 0, 2)
    smem = pl.BlockSpec(memory_space=pltpu.SMEM)
    vmem = pl.BlockSpec(memory_space=pltpu.VMEM)
    hbm = pl.BlockSpec(memory_space=pl.ANY)
    boards = subgames * rivers
    tiles, packed_tiles = slots // LANES, packed // LANES
    rows = lambda count, tile_count=tiles: pltpu.VMEM((tile_count, count, LANES), F32)
    dma = lambda *shape: pltpu.SemaphoreType.DMA(shape)
    new_trunk, new_river = pl.pallas_call(
        functools.partial(iteration_kernel, flops, turns, scale),
        out_shape=(
            jax.ShapeDtypeStruct(by_line.shape, F32),
            jax.ShapeDtypeStruct(river_regret.shape, F32),
        ),
        in_specs=[smem, smem, vmem] + [hbm] * 7,
        out_specs=(vmem, hbm),
        scratch_shapes=[
            pltpu.VMEM(river_regret.shape, F32),
            pltpu.VMEM(alive.shape, jnp.int32),
            pltpu.VMEM(ranks.shape, jnp.int32),
            pltpu.VMEM(compat.shape, BF16),
            pltpu.VMEM(cards.shape, BF16),
            pltpu.VMEM(card_slots.shape, BF16),
            pltpu.VMEM(ones.shape, BF16),
            rows(4 * boards),
            rows(4 * boards, packed_tiles),
            rows(2 * boards, packed_tiles),
            pltpu.VMEM((packed_tiles, 8, LANES), jnp.int32),
            pltpu.VMEM((tiles, 8, LANES), jnp.int32),
            rows(8),
            rows(boards, packed_tiles),
            rows(8, packed_tiles),
            pltpu.VMEM((READY, packed_tiles, packed, LANES), F8),
            rows(8 * boards, packed_tiles),
            rows(8 * boards, packed_tiles),
            rows(boards, packed_tiles),
            pltpu.VMEM((READY, 16, packed), BF16),
            pltpu.VMEM((READY, packed, LANES), BF16),
            pltpu.VMEM((16, slots), F32),
            pltpu.VMEM((16, LANES), F32),
            rows(16, turns),
            rows(8, turns),
            rows(8, turns),
            rows(8, packed_tiles),
            rows(16, flops),
            dma(7),
            pltpu.SemaphoreType.DMA,
            dma(turns),
            dma(turns),
            dma(turns),
            dma(turns),
            dma(flops),
            dma(flops),
        ],
        compiler_params=pltpu.CompilerParams(
            collective_id=0, has_side_effects=True, vmem_limit_bytes=60 * 2**20
        ),
        name="cfr_iteration",
    )(subgame_line, line_pot, by_line, river_regret, alive, ranks, compat, cards, card_slots, ones)
    return (new_trunk.transpose(1, 0, 2), new_river)


def solution(mesh):
    return jax.shard_map(
        functools.partial(on_device, mesh.shape["flop"], mesh.shape["turn"]),
        mesh=mesh,
        in_specs=(
            P(None, None, "turn"),
            P("flop", "turn", None, None, None, None),
            P(),
            P("flop"),
            P("flop", "turn", None, None),
            P("flop", "turn", None, None),
        ),
        out_specs=(P(None, None, "turn"), P("flop", "turn", None, None, None, None)),
        check_vma=False,
    )
```

```python
import functools

import jax
import jax.numpy as jnp
import numpy as np
from jax import lax
from jax.experimental import pallas as pl
from jax.experimental.pallas import tpu as pltpu
from jax.sharding import PartitionSpec as P

CARDS = 52
BET_SIZE = 2.0
LANES = 128
BLOCK = 256
READY = 8
FRESH = 6
F32 = jnp.float32
BF16 = jnp.bfloat16
F8 = jnp.float8_e4m3fn
MESH = pl.DeviceIdType.MESH


def card_pairs(slot_count, card_count=CARDS):
    first_card, second_card = np.triu_indices(card_count, 1)
    extra = slot_count - first_card.shape[0]
    pad_first = -1 - 2 * np.arange(extra)
    pad_second = -2 - 2 * np.arange(extra)
    return (
        np.concatenate([first_card, pad_first]).astype(np.int32),
        np.concatenate([second_card, pad_second]).astype(np.int32),
    )


def compat_table(slot_count, card_count):
    first, second = card_pairs(slot_count, card_count)
    collide = (
        (first[:, None] == first[None, :])
        | (first[:, None] == second[None, :])
        | (second[:, None] == first[None, :])
        | (second[:, None] == second[None, :])
        | (first[:, None] < 0)
        | (first[None, :] < 0)
    )
    return np.where(collide, 0.0, 1.0).astype(np.float32)


def card_table(slot_count, card_count):
    first, second = card_pairs(slot_count, card_count)
    cards = np.arange(LANES)[None, :]
    return ((first[:, None] == cards) | (second[:, None] == cards)).astype(np.float32)


def shifted(index, step, size):
    high = lax.rem(lax.div(index, 4) + step // 4, size // 4)
    return high * 4 + lax.rem(lax.rem(index, 4) + step % 4, 4)


def far_first(size, distances):
    high, low = distances
    return sorted(range(1, size), key=lambda step: -(high[step // 4] + low[step % 4]))


def roll_lanes(x, shift):
    shift %= x.shape[-1]
    return pltpu.roll(x, shift, 1) if shift else x


def strategy_of(regret):
    return regret / jnp.sum(regret, axis=0, keepdims=True)


def blocks_of(size):
    return [(at, min(BLOCK, size - at)) for at in range(0, size, BLOCK)]


def tiles_of(array):
    return [array[:, at : at + LANES] for at in range(0, array.shape[1], LANES)]


def rank_code(ranks):
    octave = ranks >> 7
    small = (1 << (octave & 15)).astype(F32)
    large = jnp.where(
        octave >= 32,
        jnp.where(octave >= 48, 2.0**48, 2.0**32),
        jnp.where(octave >= 16, 2.0**16, 1.0),
    )
    return ((ranks & 127) + 128).astype(F32) * small * large


def table_blocks(size):
    sides = blocks_of(size)
    return [
        (start, depth, at, width)
        for number, (start, depth) in enumerate(sides)
        for at, width in sides[number:]
    ]


def product(rows, table, axis):
    return lax.dot_general(rows, table, (((1,), (axis,)), ((), ())), preferred_element_type=F32)


def three_parts(x):
    high = x.astype(BF16)
    rest = x - high.astype(F32)
    middle = rest.astype(BF16)
    low = (rest - middle.astype(F32)).astype(BF16)
    return jnp.concatenate([high, middle, low], axis=0)


def load_rows(ref, start, count, stride=1):
    rows = pl.ds(start, count, stride=stride)
    return jnp.concatenate([ref[tile, rows, :] for tile in range(ref.shape[0])], axis=1)


def store_rows(ref, start, count, stride, value):
    rows = pl.ds(start, count, stride=stride)
    for tile, part in enumerate(tiles_of(value)):
        ref[tile, rows, :] = part


def stack_rows(rows, count):
    return jnp.broadcast_to(rows[None], (count,) + rows.shape).reshape(
        count * rows.shape[0], rows.shape[1]
    )


def lanes_at(tiles, tile, source):
    lane = source & (LANES - 1)
    at = source >> 7
    found = None
    for number in tile:
        part = jnp.take_along_axis(tiles[number], lane, axis=1)
        found = part if found is None else jnp.where(at == number, part, found)
    return found


def prefix_counts(marks, ones_ref):
    tiles = tiles_of(marks)
    inner = jnp.dot(jnp.concatenate(tiles, axis=0).astype(BF16), ones_ref[...], preferred_element_type=F32)
    base = jnp.zeros((8, 1), F32)
    counts = []
    for number, tile in enumerate(tiles):
        counts.append(inner[number * 8 : number * 8 + 8] + base)
        base = base + jnp.sum(tile, axis=1, keepdims=True)
    return jnp.concatenate(counts, axis=1).astype(jnp.int32)


def iteration_kernel(
    flops, turns, scale,
    line_hbm, pot_hbm, trunk_hbm, regret_hbm, alive_hbm, ranks_hbm, compat_hbm, cards_hbm, slots_hbm, ones_hbm,
    trunk_out, river_out,
    line_ref, pot_ref, trunk_ref, regret, alive, ranks, compat, cards, card_slots, ones, flat, sigma, fold, source, target, unblocked, open_slots,
    reach, table, left, sums, code, row_code, column_code, strategy, mine, shares, parts, pieces, values, lines_in,
    sems, out_sem, send_share, recv_share, send_part, recv_part, send_line, recv_line,
):
    flop, turn = lax.axis_index("flop"), lax.axis_index("turn")
    subgames, _, rivers, _, _, slots = regret.shape
    lines, _, share = trunk_ref.shape
    packed = compat.shape[0]
    hands = (CARDS - 4) * (CARDS - 5) // 2

    def turn_peer(step):
        return (flop, shifted(turn, step, turns))

    def flop_peer(step):
        return (shifted(flop, step, flops), turn)

    def remote(src, dst, send, recv, peer):
        return pltpu.make_async_remote_copy(
            src_ref=src, dst_ref=dst, send_sem=send, recv_sem=recv, device_id=peer, device_id_type=MESH
        )

    turn_steps = far_first(turns, ((0, 1, 2, 1), (0, 1, 1, 1)))
    flop_steps = far_first(flops, ((0, 2), (0, 1, 2, 1)))
    barrier = pltpu.get_barrier_semaphore()
    for step in turn_steps:
        pl.semaphore_signal(barrier, inc=1, device_id=turn_peer(step), device_id_type=MESH)
    for step in flop_steps:
        pl.semaphore_signal(barrier, inc=1, device_id=flop_peer(step), device_id_type=MESH)
    copies = [
        pltpu.make_async_copy(hbm, vmem, sems.at[number])
        for number, (hbm, vmem) in enumerate(
            [
                (trunk_hbm, trunk_ref),
                (line_hbm, line_ref),
                (pot_hbm, pot_ref),
                (alive_hbm, alive),
                (ones_hbm, ones),
                (ranks_hbm, ranks),
                (regret_hbm, regret),
                (cards_hbm, cards),
                (slots_hbm, card_slots),
                (compat_hbm, compat),
            ]
        )
    ]
    for copy in copies:
        copy.start()

    mine[...] = jnp.zeros_like(mine)
    copies[0].wait()
    own = [strategy_of(trunk_ref[:, player]) for player in range(2)]
    for player in range(2):
        mine[player * 8 : player * 8 + lines, :share] = own[player]
    pl.semaphore_wait(barrier, turns + flops - 2)
    sent = []
    for step in turn_steps:
        sent.append(
            remote(mine, shares.at[turn], send_share.at[step], recv_share.at[turn], turn_peer(step))
        )
        sent[-1].start()
    shares[turn] = mine[...]

    copies[3].wait()
    copies[4].wait()
    rows = [jnp.max(alive[s, 0].astype(F32), axis=0, keepdims=True) for s in range(subgames)]
    live_any = jnp.concatenate(rows + rows, axis=0)
    before = prefix_counts(1.0 - live_any, ones)
    slot = lax.broadcasted_iota(jnp.int32, (8, slots), 1)
    state = jnp.where(live_any > 0.5, before * 2048 + slot, 0)
    for bit in range(8):
        moved = pltpu.roll(state, slots - (1 << bit), 1)
        flag = 2048 << bit
        state = jnp.where((moved & flag) != 0, moved, jnp.where((state & flag) != 0, 0, state))
    store_rows(target, 0, 8, 1, slot - before)
    store_rows(unblocked, 0, 8, 1, live_any)
    store_rows(source, 0, 8, 1, (state & 2047)[:, :packed])

    def spread(ref, subgame):
        return [
            jnp.broadcast_to(ref[tile, pl.ds(subgame, 1), :], (8, LANES))
            for tile in range(ref.shape[0])
        ]

    def pack(tiles, sources):
        return jnp.concatenate(
            [lanes_at(tiles, (t, t + 1, t + 2), sources[t]) for t in range(packed // LANES)], axis=1
        )

    def unpack(tiles, targets):
        found = []
        for t in range(slots // LANES):
            near = [n for n in (t - 2, t - 1, t) if 0 <= n < packed // LANES]
            found.append(lanes_at(tiles, near, targets[t]))
        return jnp.concatenate(found, axis=1)

    for number in (1, 2, 5, 6, 7, 8):
        copies[number].wait()

    def rounded(x):
        return x.astype(BF16).astype(F32)

    def prepare(subgame, carry):
        sources = spread(source, subgame)
        first = pl.multiple_of(subgame * rivers, rivers)
        base = pl.multiple_of(subgame * 4 * rivers, 4 * rivers)
        store_rows(code, first, rivers, 1, pack(tiles_of(rank_code(ranks[subgame, 0])), sources))
        for river in range(rivers):
            for player in range(2):
                store_rows(flat, base + river * 4 + player * 2, 2, 1, regret[subgame, 0, river, player])
        one_check, one_bet, two_fold, two_call = [
            pack(tiles_of(load_rows(flat, base + n, rivers, 4)), sources) for n in range(4)
        ]
        one_sum = one_check + one_bet
        two_sum = two_fold + two_call
        for number, part in enumerate(
            [one_check / one_sum, one_bet / one_sum, two_fold / two_sum, two_call / two_sum]
        ):
            store_rows(sigma, base + number, rivers, 4, part)
        at = lax.broadcasted_iota(jnp.int32, (rivers, packed), 1)
        live = pack(tiles_of(alive[subgame, 0].astype(F32)), sources)
        store_rows(open_slots, first, rivers, 1, jnp.where(at < hands, live, 0.0))
        return carry

    lax.fori_loop(0, subgames, prepare, 0)
    copies[9].wait()

    blocks = table_blocks(packed)

    def ready_codes(first, count):
        for which in range(count):
            codes = load_rows(code, first + which, 1)
            row_code[which] = jnp.broadcast_to(codes, (16, packed)).astype(BF16)
            tall = jnp.broadcast_to(codes, (LANES, packed)).astype(BF16)
            for at in range(0, packed, LANES):
                column_code[which, at : at + LANES, :] = jnp.transpose(tall[:, at : at + LANES])

    def sign_block(which, block, most):
        start, depth, at, width = block
        one = jnp.ones((), BF16)
        column = column_code[which, start : start + depth, :]
        column = jnp.concatenate([column] * (width // LANES), axis=1)
        row = stack_rows(row_code[which, :, at : at + width], depth // 16)
        return (jnp.maximum(jnp.minimum(row - column, one), -one) * most).astype(F8)

    def masks(block):
        start, depth, at, width = block
        return compat[start : start + depth, at : at + width]

    def play(boards, sign_of):
        lefts = [load_rows(left, pl.multiple_of(board * 8, 8), 8).astype(BF16) for board in boards]
        totals = {}

        def add(which, at, part):
            for number, piece in enumerate(tiles_of(part)):
                key = (which, at // LANES + number)
                totals[key] = totals[key] + piece if key in totals else piece

        for block in blocks:
            start, depth, at, width = block
            most = masks(block)
            for which in range(len(boards)):
                sign = sign_of(which, block, most)
                add(which, at, product(lefts[which][:, start : start + depth], sign, 0))
                if at > start:
                    add(which, start, -product(lefts[which][:, at : at + width], sign, 1))
        for which, board in enumerate(boards):
            rows = pl.ds(pl.multiple_of(board * 8, 8), 8)
            for number in range(packed // LANES):
                sums[number, rows, :] = totals[which, number]

    def tables(block):
        start, depth, at, width = block
        return [(slice(start, start + depth), at // LANES + n) for n in range(width // LANES)]

    def build_first():
        ready_codes(0, READY)
        for block in blocks:
            most = masks(block)
            for which in range(READY):
                for (rows, tile), part in zip(tables(block), tiles_of(sign_block(which, block, most))):
                    table[which, tile, rows, :] = part

    def built(which, block):
        return jnp.concatenate([table[which, tile, rows, :] for rows, tile in tables(block)], axis=1)

    steps = (subgames * rivers - READY) // FRESH
    ready = READY // steps

    def add_folds(subgame):
        start = pl.multiple_of(subgame * 8 * rivers, 8 * rivers)
        fold_in = jnp.concatenate([load_rows(left, start + n, rivers, 8) for n in (4, 2)], axis=0)
        per_card = jnp.dot(fold_in.astype(BF16), cards[...], preferred_element_type=F32)
        per_slot = jnp.dot(three_parts(per_card), card_slots[...], preferred_element_type=F32)
        count = fold_in.shape[0]
        per_slot = per_slot[:count] + per_slot[count : 2 * count] + per_slot[2 * count :]
        fold_sums = jnp.sum(fold_in, axis=1, keepdims=True) - per_slot + fold_in
        store_rows(fold, pl.multiple_of(subgame * 2 * rivers, 2 * rivers), 2 * rivers, 1, fold_sums)

    def some_boards(step, carry):
        for number in range(subgames // steps):
            add_folds(step * (subgames // steps) + number)
        first = READY + step * FRESH
        ready_codes(first, FRESH)

        def sign_of(which, block, most):
            if which < FRESH:
                return sign_block(which, block, most)
            return built(step * ready + which - FRESH, block)

        play([first + n for n in range(FRESH)] + [step * ready + n for n in range(ready)], sign_of)
        return carry

    build_first()

    for step in turn_steps:
        peer = turn_peer(step)
        remote(mine, shares.at[peer[1]], send_share.at[step], recv_share.at[peer[1]], peer).wait_recv()
    lane = lax.broadcasted_iota(jnp.int32, (16, LANES), 1)
    tiles = [None] * (slots // LANES)
    for number in range(turns):
        tile, offset = divmod(number * share, LANES)
        piece = roll_lanes(shares[number], offset)
        low = jnp.where(lane >= offset, piece, 0.0) if offset else piece
        tiles[tile] = low if tiles[tile] is None else tiles[tile] + low
        if offset + share > LANES:
            tiles[tile + 1] = jnp.where(lane < offset + share - LANES, piece, 0.0)
    for tile, value in enumerate(tiles):
        strategy[:, tile * LANES : (tile + 1) * LANES] = value
    chosen = [
        strategy[pl.ds(8 * player + line_ref[subgame], 1), :]
        for player in range(2)
        for subgame in range(subgames)
    ]
    chosen = tiles_of(jnp.concatenate(chosen, axis=0))
    store_rows(reach, 0, 8, 1, pack(chosen, [source[t] for t in range(packed // LANES)]))

    def enter(subgame, carry):
        first = pl.multiple_of(subgame * rivers, rivers)
        base = pl.multiple_of(subgame * 4 * rivers, 4 * rivers)
        reach_one = load_rows(reach, subgame, 1)
        reach_two = load_rows(reach, subgames + subgame, 1)
        live = load_rows(open_slots, first, rivers)
        sigma_check, sigma_bet, sigma_fold, sigma_call = [
            load_rows(sigma, base + n, rivers, 4) for n in range(4)
        ]
        in_bet = rounded(live * (reach_one * sigma_bet))
        in_fold = rounded(live * (reach_two * sigma_fold))
        shows = [
            live * reach_two,
            live * (reach_two * sigma_call),
            in_bet,
            live * (reach_one * sigma_check),
        ]
        start = pl.multiple_of(subgame * 8 * rivers, 8 * rivers)
        none = jnp.zeros((rivers, packed), F32)
        for number, value in enumerate(shows + [in_fold, none, none, none]):
            store_rows(left, start + number, rivers, 8, value)
        return carry

    lax.fori_loop(0, subgames, enter, 0)

    lax.fori_loop(0, steps, some_boards, 0)

    def leave(subgame, carry):
        first = pl.multiple_of(subgame * rivers, rivers)
        base = pl.multiple_of(subgame * 4 * rivers, 4 * rivers)
        start = pl.multiple_of(subgame * 8 * rivers, 8 * rivers)
        half_pot = 0.5 * pot_ref[line_ref[subgame]]
        call_pot = half_pot + BET_SIZE
        live = load_rows(open_slots, first, rivers)
        weight = live * (1.0 / ((CARDS - 7) * (CARDS - 8) / 2.0))
        show = [load_rows(sums, start + number, rivers, 8) * weight for number in range(4)]
        fold_sums = load_rows(fold, pl.multiple_of(subgame * 2 * rivers, 2 * rivers), 2 * rivers)
        fold_two, fold_one = fold_sums[:rivers] * weight, fold_sums[rivers:] * weight
        sigma_check, sigma_bet, sigma_fold, sigma_call = [
            load_rows(sigma, base + n, rivers, 4) for n in range(4)
        ]
        check_value = half_pot * show[0]
        bet_value = half_pot * fold_two + call_pot * show[1]
        fold_value = -half_pot * fold_one
        call_value = call_pot * show[2]
        check_line = half_pot * show[3]
        one_node = sigma_check * check_value + sigma_bet * bet_value
        two_node = sigma_fold * fold_value + sigma_call * call_value
        for number, value in enumerate(
            [check_value - one_node, bet_value - one_node, fold_value - two_node, call_value - two_node]
        ):
            store_rows(sigma, base + number, rivers, 4, value)
        roots = [
            jnp.sum(one_node, axis=0, keepdims=True),
            jnp.sum(check_line + two_node, axis=0, keepdims=True),
        ]
        for player in range(2):
            store_rows(values, player * subgames + subgame, 1, 1, roots[player])
        return carry

    lax.fori_loop(0, subgames, leave, 0)

    lane = lax.broadcasted_iota(jnp.int32, (8, LANES), 1)
    roots = [values[t] for t in range(packed // LANES)]
    roots = tiles_of(unpack(roots, [target[t] for t in range(slots // LANES)]))
    roots = [part * unblocked[t] for t, part in enumerate(roots)]
    for number in range(turns):
        tile, offset = divmod(number * share, LANES)
        piece = roll_lanes(roots[tile], -offset)
        if offset + share > LANES:
            after = roll_lanes(roots[tile + 1], -offset)
            piece = jnp.where(lane < LANES - offset, piece, after)
        parts[number] = piece
    for step in turn_steps:
        peer = turn_peer(step)
        sent.append(
            remote(parts.at[peer[1]], pieces.at[turn], send_part.at[step], recv_part.at[turn], peer)
        )
        sent[-1].start()
    pieces[turn] = parts[turn]

    def write(subgame, carry):
        targets = spread(target, subgame)
        base = pl.multiple_of(subgame * 4 * rivers, 4 * rivers)
        live = alive[subgame, 0].astype(F32)
        for number in range(4):
            change = unpack(tiles_of(load_rows(sigma, base + number, rivers, 4)), targets) * live
            value = jnp.maximum(load_rows(flat, base + number, rivers, 4) + change, 0.0)
            store_rows(flat, base + number, rivers, 4, value)
        for river in range(rivers):
            for player in range(2):
                regret[subgame, 0, river, player] = load_rows(flat, base + river * 4 + player * 2, 2)
        return carry

    lax.fori_loop(0, subgames, write, 0)
    out_copy = pltpu.make_async_copy(regret, river_out, out_sem)
    out_copy.start()

    for step in turn_steps:
        peer = turn_peer(step)
        remote(
            parts.at[peer[1]], pieces.at[peer[1]], send_part.at[step], recv_part.at[peer[1]], peer
        ).wait_recv()
    root = pieces[0]
    for number in range(1, turns):
        root = root + pieces[number]
    row = lax.broadcasted_iota(jnp.int32, (8, LANES), 0)
    for player in range(2):
        by_line = jnp.zeros((8, LANES), F32)
        for subgame in range(subgames):
            at = player * subgames + subgame
            by_line = by_line + jnp.where(row == line_ref[subgame], root[at : at + 1, :], 0.0)
        mine_lines = lines_in.at[flop]
        mine_lines[player * 8 : player * 8 + 8, :] = by_line
    for step in flop_steps:
        sent.append(
            remote(
                lines_in.at[flop], lines_in.at[flop], send_line.at[step], recv_line.at[flop], flop_peer(step)
            )
        )
        sent[-1].start()
    for step in flop_steps:
        peer = flop_peer(step)
        remote(
            lines_in.at[flop], lines_in.at[peer[0]], send_line.at[step], recv_line.at[peer[0]], peer
        ).wait_recv()
    total = lines_in[0]
    for number in range(1, flops):
        total = total + lines_in[number]
    total = total * scale
    for player in range(2):
        line_values = total[player * 8 : player * 8 + lines, :share]
        node = jnp.sum(own[player] * line_values, axis=0, keepdims=True)
        trunk_out[:, player] = jnp.maximum(trunk_ref[:, player] + line_values - node, 0.0)
    out_copy.wait()
    for copy in sent:
        copy.wait_send()


def on_device(flops, turns, trunk_regret, river_regret, line_pot, subgame_line, alive, ranks):
    subgames, turn_local, rivers, _, _, slots = river_regret.shape
    lines = trunk_regret.shape[1]
    scale = lines / (subgames * flops * turn_local * turns * rivers)
    packed = -(-((CARDS - 4) * (CARDS - 5) // 2) // LANES) * LANES
    compat = jnp.asarray(compat_table(packed, CARDS - 4).astype(jnp.bfloat16))
    cards = jnp.asarray(card_table(packed, CARDS - 4).astype(jnp.bfloat16))
    card_slots = jnp.asarray(card_table(packed, CARDS - 4).T.astype(jnp.bfloat16))
    ones = jnp.asarray(np.triu(np.ones((LANES, LANES)), 1).astype(jnp.bfloat16))
    by_line = trunk_regret.transpose(1, 0, 2)
    vmem = pl.BlockSpec(memory_space=pltpu.VMEM)
    hbm = pl.BlockSpec(memory_space=pl.ANY)
    boards = subgames * rivers
    tiles, packed_tiles = slots // LANES, packed // LANES
    rows = lambda count, tile_count=tiles: pltpu.VMEM((tile_count, count, LANES), F32)
    dma = lambda *shape: pltpu.SemaphoreType.DMA(shape)
    new_trunk, new_river = pl.pallas_call(
        functools.partial(iteration_kernel, flops, turns, scale),
        out_shape=(
            jax.ShapeDtypeStruct(by_line.shape, F32),
            jax.ShapeDtypeStruct(river_regret.shape, F32),
        ),
        in_specs=[hbm] * 10,
        out_specs=(vmem, hbm),
        scratch_shapes=[
            pltpu.SMEM(subgame_line.shape, jnp.int32),
            pltpu.SMEM(line_pot.shape, F32),
            pltpu.VMEM(by_line.shape, F32),
            pltpu.VMEM(river_regret.shape, F32),
            pltpu.VMEM(alive.shape, jnp.int32),
            pltpu.VMEM(ranks.shape, jnp.int32),
            pltpu.VMEM(compat.shape, BF16),
            pltpu.VMEM(cards.shape, BF16),
            pltpu.VMEM(card_slots.shape, BF16),
            pltpu.VMEM(ones.shape, BF16),
            rows(4 * boards),
            rows(4 * boards, packed_tiles),
            rows(2 * boards, packed_tiles),
            pltpu.VMEM((packed_tiles, 8, LANES), jnp.int32),
            pltpu.VMEM((tiles, 8, LANES), jnp.int32),
            rows(8),
            rows(boards, packed_tiles),
            rows(8, packed_tiles),
            pltpu.VMEM((READY, packed_tiles, packed, LANES), F8),
            rows(8 * boards, packed_tiles),
            rows(8 * boards, packed_tiles),
            rows(boards, packed_tiles),
            pltpu.VMEM((READY, 16, packed), BF16),
            pltpu.VMEM((READY, packed, LANES), BF16),
            pltpu.VMEM((16, slots), F32),
            pltpu.VMEM((16, LANES), F32),
            rows(16, turns),
            rows(8, turns),
            rows(8, turns),
            rows(8, packed_tiles),
            rows(16, flops),
            dma(10),
            pltpu.SemaphoreType.DMA,
            dma(turns),
            dma(turns),
            dma(turns),
            dma(turns),
            dma(flops),
            dma(flops),
        ],
        compiler_params=pltpu.CompilerParams(
            collective_id=0, has_side_effects=True, vmem_limit_bytes=60 * 2**20
        ),
        name="cfr_iteration",
    )(subgame_line, line_pot, by_line, river_regret, alive, ranks, compat, cards, card_slots, ones)
    return (new_trunk.transpose(1, 0, 2), new_river)


def solution(mesh):
    return jax.shard_map(
        functools.partial(on_device, mesh.shape["flop"], mesh.shape["turn"]),
        mesh=mesh,
        in_specs=(
            P(None, None, "turn"),
            P("flop", "turn", None, None, None, None),
            P(),
            P("flop"),
            P("flop", "turn", None, None),
            P("flop", "turn", None, None),
        ),
        out_specs=(P(None, None, "turn"), P("flop", "turn", None, None, None, None)),
        check_vma=False,
    )
```

```python
import functools

import jax
import jax.numpy as jnp
import numpy as np
from jax import lax
from jax.experimental import pallas as pl
from jax.experimental.pallas import tpu as pltpu
from jax.sharding import PartitionSpec as P

CARDS = 52
BET_SIZE = 2.0
LANES = 128
BLOCK = 256
READY = 8
FRESH = 6
F32 = jnp.float32
BF16 = jnp.bfloat16
F8 = jnp.float8_e4m3fn
MESH = pl.DeviceIdType.MESH


def card_pairs(slot_count, card_count=CARDS):
    first_card, second_card = np.triu_indices(card_count, 1)
    extra = slot_count - first_card.shape[0]
    pad_first = -1 - 2 * np.arange(extra)
    pad_second = -2 - 2 * np.arange(extra)
    return (
        np.concatenate([first_card, pad_first]).astype(np.int32),
        np.concatenate([second_card, pad_second]).astype(np.int32),
    )


def compat_table(slot_count, card_count):
    first, second = card_pairs(slot_count, card_count)
    collide = (
        (first[:, None] == first[None, :])
        | (first[:, None] == second[None, :])
        | (second[:, None] == first[None, :])
        | (second[:, None] == second[None, :])
        | (first[:, None] < 0)
        | (first[None, :] < 0)
    )
    return np.where(collide, 0.0, 1.0).astype(np.float32)


def card_table(slot_count, card_count):
    first, second = card_pairs(slot_count, card_count)
    cards = np.arange(LANES)[None, :]
    return ((first[:, None] == cards) | (second[:, None] == cards)).astype(np.float32)


def shifted(index, step, size):
    high = lax.rem(lax.div(index, 4) + step // 4, size // 4)
    return high * 4 + lax.rem(lax.rem(index, 4) + step % 4, 4)


def far_first(size, distances):
    high, low = distances
    return sorted(range(1, size), key=lambda step: -(high[step // 4] + low[step % 4]))


def roll_lanes(x, shift):
    shift %= x.shape[-1]
    return pltpu.roll(x, shift, 1) if shift else x


def strategy_of(regret):
    return regret / jnp.sum(regret, axis=0, keepdims=True)


def blocks_of(size):
    return [(at, min(BLOCK, size - at)) for at in range(0, size, BLOCK)]


def tiles_of(array):
    return [array[:, at : at + LANES] for at in range(0, array.shape[1], LANES)]


def rank_code(ranks):
    octave = ranks >> 7
    small = (1 << (octave & 15)).astype(F32)
    large = jnp.where(
        octave >= 32,
        jnp.where(octave >= 48, 2.0**48, 2.0**32),
        jnp.where(octave >= 16, 2.0**16, 1.0),
    )
    return ((ranks & 127) + 128).astype(F32) * small * large


def table_blocks(size):
    sides = blocks_of(size)
    return [
        (start, depth, at, width)
        for number, (start, depth) in enumerate(sides)
        for at, width in sides[number:]
    ]


def product(rows, table, axis):
    return lax.dot_general(rows, table, (((1,), (axis,)), ((), ())), preferred_element_type=F32)


def three_parts(x):
    high = x.astype(BF16)
    rest = x - high.astype(F32)
    middle = rest.astype(BF16)
    low = (rest - middle.astype(F32)).astype(BF16)
    return jnp.concatenate([high, middle, low], axis=0)


def load_rows(ref, start, count, stride=1):
    rows = pl.ds(start, count, stride=stride)
    return jnp.concatenate([ref[tile, rows, :] for tile in range(ref.shape[0])], axis=1)


def store_rows(ref, start, count, stride, value):
    rows = pl.ds(start, count, stride=stride)
    for tile, part in enumerate(tiles_of(value)):
        ref[tile, rows, :] = part


def stack_rows(rows, count):
    return jnp.broadcast_to(rows[None], (count,) + rows.shape).reshape(
        count * rows.shape[0], rows.shape[1]
    )


def lanes_at(tiles, tile, source):
    lane = source & (LANES - 1)
    at = source >> 7
    found = None
    for number in tile:
        part = jnp.take_along_axis(tiles[number], lane, axis=1)
        found = part if found is None else jnp.where(at == number, part, found)
    return found


def prefix_counts(marks, ones_ref):
    tiles = tiles_of(marks)
    inner = jnp.dot(jnp.concatenate(tiles, axis=0).astype(BF16), ones_ref[...], preferred_element_type=F32)
    base = jnp.zeros((8, 1), F32)
    counts = []
    for number, tile in enumerate(tiles):
        counts.append(inner[number * 8 : number * 8 + 8] + base)
        base = base + jnp.sum(tile, axis=1, keepdims=True)
    return jnp.concatenate(counts, axis=1).astype(jnp.int32)


def iteration_kernel(
    flops, turns, scale,
    line_hbm, pot_hbm, trunk_hbm, regret_hbm, alive_hbm, ranks_hbm, compat_hbm, cards_hbm, slots_hbm, ones_hbm,
    trunk_out, river_out,
    line_ref, pot_ref, trunk_ref, regret, alive, ranks, compat, cards, card_slots, ones, flat, sigma, fold, source, target, unblocked, open_slots,
    reach, table, left, sums, code, row_code, column_code, strategy, mine, shares, parts, pieces, values, lines_in,
    sems, out_sem, send_share, recv_share, send_part, recv_part, send_line, recv_line,
):
    flop, turn = lax.axis_index("flop"), lax.axis_index("turn")
    subgames, _, rivers, _, _, slots = regret.shape
    lines, _, share = trunk_ref.shape
    packed = compat.shape[0]
    hands = (CARDS - 4) * (CARDS - 5) // 2

    def turn_peer(step):
        return (flop, shifted(turn, step, turns))

    def flop_peer(step):
        return (shifted(flop, step, flops), turn)

    def remote(src, dst, send, recv, peer):
        return pltpu.make_async_remote_copy(
            src_ref=src, dst_ref=dst, send_sem=send, recv_sem=recv, device_id=peer, device_id_type=MESH
        )

    turn_steps = far_first(turns, ((0, 1, 2, 1), (0, 1, 1, 1)))
    flop_steps = far_first(flops, ((0, 2), (0, 1, 2, 1)))
    barrier = pltpu.get_barrier_semaphore()
    for step in turn_steps:
        pl.semaphore_signal(barrier, inc=1, device_id=turn_peer(step), device_id_type=MESH)
    for step in flop_steps:
        pl.semaphore_signal(barrier, inc=1, device_id=flop_peer(step), device_id_type=MESH)
    copies = [
        pltpu.make_async_copy(hbm, vmem, sems.at[number])
        for number, (hbm, vmem) in enumerate(
            [
                (trunk_hbm, trunk_ref),
                (line_hbm, line_ref),
                (pot_hbm, pot_ref),
                (alive_hbm, alive),
                (ones_hbm, ones),
                (ranks_hbm, ranks),
                (regret_hbm, regret),
                (cards_hbm, cards),
                (slots_hbm, card_slots),
                (compat_hbm, compat),
            ]
        )
    ]
    for copy in copies:
        copy.start()

    mine[...] = jnp.zeros_like(mine)
    copies[0].wait()
    own = [strategy_of(trunk_ref[:, player]) for player in range(2)]
    for player in range(2):
        mine[player * 8 : player * 8 + lines, :share] = own[player]
    pl.semaphore_wait(barrier, turns + flops - 2)
    sent = []
    for step in turn_steps:
        sent.append(
            remote(mine, shares.at[turn], send_share.at[step], recv_share.at[turn], turn_peer(step))
        )
        sent[-1].start()
    shares[turn] = mine[...]

    copies[3].wait()
    copies[4].wait()
    rows = [jnp.max(alive[s, 0].astype(F32), axis=0, keepdims=True) for s in range(subgames)]
    live_any = jnp.concatenate(rows + rows, axis=0)
    before = prefix_counts(1.0 - live_any, ones)
    slot = lax.broadcasted_iota(jnp.int32, (8, slots), 1)
    state = jnp.where(live_any > 0.5, before * 2048 + slot, 0)
    for bit in range(8):
        moved = pltpu.roll(state, slots - (1 << bit), 1)
        flag = 2048 << bit
        state = jnp.where((moved & flag) != 0, moved, jnp.where((state & flag) != 0, 0, state))
    store_rows(target, 0, 8, 1, slot - before)
    store_rows(unblocked, 0, 8, 1, live_any)
    store_rows(source, 0, 8, 1, (state & 2047)[:, :packed])

    def spread(ref, subgame):
        return [
            jnp.broadcast_to(ref[tile, pl.ds(subgame, 1), :], (8, LANES))
            for tile in range(ref.shape[0])
        ]

    def pack(tiles, sources):
        return jnp.concatenate(
            [lanes_at(tiles, (t, t + 1, t + 2), sources[t]) for t in range(packed // LANES)], axis=1
        )

    def unpack(tiles, targets):
        found = []
        for t in range(slots // LANES):
            near = [n for n in (t - 2, t - 1, t) if 0 <= n < packed // LANES]
            found.append(lanes_at(tiles, near, targets[t]))
        return jnp.concatenate(found, axis=1)

    for number in (1, 2, 5, 6, 7, 8):
        copies[number].wait()

    def rounded(x):
        return x.astype(BF16).astype(F32)

    def prepare(subgame, carry):
        sources = spread(source, subgame)
        first = pl.multiple_of(subgame * rivers, rivers)
        base = pl.multiple_of(subgame * 4 * rivers, 4 * rivers)
        store_rows(code, first, rivers, 1, pack(tiles_of(rank_code(ranks[subgame, 0])), sources))
        for river in range(rivers):
            for player in range(2):
                store_rows(flat, base + river * 4 + player * 2, 2, 1, regret[subgame, 0, river, player])
        one_check, one_bet, two_fold, two_call = [
            pack(tiles_of(load_rows(flat, base + n, rivers, 4)), sources) for n in range(4)
        ]
        one_sum = one_check + one_bet
        two_sum = two_fold + two_call
        for number, part in enumerate(
            [one_check / one_sum, one_bet / one_sum, two_fold / two_sum, two_call / two_sum]
        ):
            store_rows(sigma, base + number, rivers, 4, part)
        at = lax.broadcasted_iota(jnp.int32, (rivers, packed), 1)
        live = pack(tiles_of(alive[subgame, 0].astype(F32)), sources)
        store_rows(open_slots, first, rivers, 1, jnp.where(at < hands, live, 0.0))
        return carry

    lax.fori_loop(0, subgames, prepare, 0)
    copies[9].wait()

    blocks = table_blocks(packed)

    def ready_codes(first, count):
        for which in range(count):
            codes = load_rows(code, first + which, 1)
            row_code[which] = jnp.broadcast_to(codes, (16, packed)).astype(BF16)
            tall = jnp.broadcast_to(codes, (LANES, packed)).astype(BF16)
            for at in range(0, packed, LANES):
                column_code[which, at : at + LANES, :] = jnp.transpose(tall[:, at : at + LANES])

    def sign_block(which, block, most):
        start, depth, at, width = block
        one = jnp.ones((), BF16)
        column = column_code[which, start : start + depth, :]
        column = jnp.concatenate([column] * (width // LANES), axis=1)
        row = stack_rows(row_code[which, :, at : at + width], depth // 16)
        return (jnp.maximum(jnp.minimum(row - column, one), -one) * most).astype(F8)

    def masks(block):
        start, depth, at, width = block
        return compat[start : start + depth, at : at + width]

    def play(boards, sign_of):
        lefts = [load_rows(left, pl.multiple_of(board * 8, 8), 8).astype(BF16) for board in boards]
        totals = {}

        def add(which, at, part):
            for number, piece in enumerate(tiles_of(part)):
                key = (which, at // LANES + number)
                totals[key] = totals[key] + piece if key in totals else piece

        for block in blocks:
            start, depth, at, width = block
            most = masks(block)
            for which in range(len(boards)):
                sign = sign_of(which, block, most)
                add(which, at, product(lefts[which][:, start : start + depth], sign, 0))
                if at > start:
                    add(which, start, -product(lefts[which][:, at : at + width], sign, 1))
        for which, board in enumerate(boards):
            rows = pl.ds(pl.multiple_of(board * 8, 8), 8)
            for number in range(packed // LANES):
                sums[number, rows, :] = totals[which, number]

    def tables(block):
        start, depth, at, width = block
        return [(slice(start, start + depth), at // LANES + n) for n in range(width // LANES)]

    def build_first():
        ready_codes(0, READY)
        for block in blocks:
            most = masks(block)
            for which in range(READY):
                for (rows, tile), part in zip(tables(block), tiles_of(sign_block(which, block, most))):
                    table[which, tile, rows, :] = part

    def built(which, block):
        return jnp.concatenate([table[which, tile, rows, :] for rows, tile in tables(block)], axis=1)

    steps = (subgames * rivers - READY) // FRESH
    ready = READY // steps

    def add_folds(subgame):
        start = pl.multiple_of(subgame * 8 * rivers, 8 * rivers)
        fold_in = jnp.concatenate([load_rows(left, start + n, rivers, 8) for n in (4, 2)], axis=0)
        per_card = jnp.dot(fold_in.astype(BF16), cards[...], preferred_element_type=F32)
        per_slot = jnp.dot(three_parts(per_card), card_slots[...], preferred_element_type=F32)
        count = fold_in.shape[0]
        per_slot = per_slot[:count] + per_slot[count : 2 * count] + per_slot[2 * count :]
        fold_sums = jnp.sum(fold_in, axis=1, keepdims=True) - per_slot + fold_in
        store_rows(fold, pl.multiple_of(subgame * 2 * rivers, 2 * rivers), 2 * rivers, 1, fold_sums)

    def some_boards(step, carry):
        for number in range(subgames // steps):
            add_folds(step * (subgames // steps) + number)
        first = READY + step * FRESH
        ready_codes(first, FRESH)

        def sign_of(which, block, most):
            if which < FRESH:
                return sign_block(which, block, most)
            return built(step * ready + which - FRESH, block)

        play([first + n for n in range(FRESH)] + [step * ready + n for n in range(ready)], sign_of)
        return carry

    build_first()

    for step in turn_steps:
        peer = turn_peer(step)
        remote(mine, shares.at[peer[1]], send_share.at[step], recv_share.at[peer[1]], peer).wait_recv()
    lane = lax.broadcasted_iota(jnp.int32, (16, LANES), 1)
    tiles = [None] * (slots // LANES)
    for number in range(turns):
        tile, offset = divmod(number * share, LANES)
        piece = roll_lanes(shares[number], offset)
        low = jnp.where(lane >= offset, piece, 0.0) if offset else piece
        tiles[tile] = low if tiles[tile] is None else tiles[tile] + low
        if offset + share > LANES:
            tiles[tile + 1] = jnp.where(lane < offset + share - LANES, piece, 0.0)
    for tile, value in enumerate(tiles):
        strategy[:, tile * LANES : (tile + 1) * LANES] = value
    chosen = [
        strategy[pl.ds(8 * player + line_ref[subgame], 1), :]
        for player in range(2)
        for subgame in range(subgames)
    ]
    chosen = tiles_of(jnp.concatenate(chosen, axis=0))
    store_rows(reach, 0, 8, 1, pack(chosen, [source[t] for t in range(packed // LANES)]))

    def enter(subgame, carry):
        first = pl.multiple_of(subgame * rivers, rivers)
        base = pl.multiple_of(subgame * 4 * rivers, 4 * rivers)
        reach_one = load_rows(reach, subgame, 1)
        reach_two = load_rows(reach, subgames + subgame, 1)
        live = load_rows(open_slots, first, rivers)
        sigma_check, sigma_bet, sigma_fold, sigma_call = [
            load_rows(sigma, base + n, rivers, 4) for n in range(4)
        ]
        in_bet = rounded(live * (reach_one * sigma_bet))
        in_fold = rounded(live * (reach_two * sigma_fold))
        shows = [
            live * reach_two,
            live * (reach_two * sigma_call),
            in_bet,
            live * (reach_one * sigma_check),
        ]
        start = pl.multiple_of(subgame * 8 * rivers, 8 * rivers)
        none = jnp.zeros((rivers, packed), F32)
        for number, value in enumerate(shows + [in_fold, none, none, none]):
            store_rows(left, start + number, rivers, 8, value)
        return carry

    lax.fori_loop(0, subgames, enter, 0, unroll=True)

    lax.fori_loop(0, steps, some_boards, 0)

    def leave(subgame, carry):
        first = pl.multiple_of(subgame * rivers, rivers)
        base = pl.multiple_of(subgame * 4 * rivers, 4 * rivers)
        start = pl.multiple_of(subgame * 8 * rivers, 8 * rivers)
        half_pot = 0.5 * pot_ref[line_ref[subgame]]
        call_pot = half_pot + BET_SIZE
        live = load_rows(open_slots, first, rivers)
        weight = live * (1.0 / ((CARDS - 7) * (CARDS - 8) / 2.0))
        show = [load_rows(sums, start + number, rivers, 8) * weight for number in range(4)]
        fold_sums = load_rows(fold, pl.multiple_of(subgame * 2 * rivers, 2 * rivers), 2 * rivers)
        fold_two, fold_one = fold_sums[:rivers] * weight, fold_sums[rivers:] * weight
        sigma_check, sigma_bet, sigma_fold, sigma_call = [
            load_rows(sigma, base + n, rivers, 4) for n in range(4)
        ]
        check_value = half_pot * show[0]
        bet_value = half_pot * fold_two + call_pot * show[1]
        fold_value = -half_pot * fold_one
        call_value = call_pot * show[2]
        check_line = half_pot * show[3]
        one_node = sigma_check * check_value + sigma_bet * bet_value
        two_node = sigma_fold * fold_value + sigma_call * call_value
        for number, value in enumerate(
            [check_value - one_node, bet_value - one_node, fold_value - two_node, call_value - two_node]
        ):
            store_rows(sigma, base + number, rivers, 4, value)
        roots = [
            jnp.sum(one_node, axis=0, keepdims=True),
            jnp.sum(check_line + two_node, axis=0, keepdims=True),
        ]
        for player in range(2):
            store_rows(values, player * subgames + subgame, 1, 1, roots[player])
        return carry

    lax.fori_loop(0, subgames, leave, 0, unroll=True)

    lane = lax.broadcasted_iota(jnp.int32, (8, LANES), 1)
    roots = [values[t] for t in range(packed // LANES)]
    roots = tiles_of(unpack(roots, [target[t] for t in range(slots // LANES)]))
    roots = [part * unblocked[t] for t, part in enumerate(roots)]
    for number in range(turns):
        tile, offset = divmod(number * share, LANES)
        piece = roll_lanes(roots[tile], -offset)
        if offset + share > LANES:
            after = roll_lanes(roots[tile + 1], -offset)
            piece = jnp.where(lane < LANES - offset, piece, after)
        parts[number] = piece
    for step in turn_steps:
        peer = turn_peer(step)
        sent.append(
            remote(parts.at[peer[1]], pieces.at[turn], send_part.at[step], recv_part.at[turn], peer)
        )
        sent[-1].start()
    pieces[turn] = parts[turn]

    def write(subgame, carry):
        targets = spread(target, subgame)
        base = pl.multiple_of(subgame * 4 * rivers, 4 * rivers)
        live = alive[subgame, 0].astype(F32)
        for number in range(4):
            change = unpack(tiles_of(load_rows(sigma, base + number, rivers, 4)), targets) * live
            value = jnp.maximum(load_rows(flat, base + number, rivers, 4) + change, 0.0)
            store_rows(flat, base + number, rivers, 4, value)
        for river in range(rivers):
            for player in range(2):
                regret[subgame, 0, river, player] = load_rows(flat, base + river * 4 + player * 2, 2)
        return carry

    lax.fori_loop(0, subgames, write, 0)
    out_copy = pltpu.make_async_copy(regret, river_out, out_sem)
    out_copy.start()

    for step in turn_steps:
        peer = turn_peer(step)
        remote(
            parts.at[peer[1]], pieces.at[peer[1]], send_part.at[step], recv_part.at[peer[1]], peer
        ).wait_recv()
    root = pieces[0]
    for number in range(1, turns):
        root = root + pieces[number]
    row = lax.broadcasted_iota(jnp.int32, (8, LANES), 0)
    for player in range(2):
        by_line = jnp.zeros((8, LANES), F32)
        for subgame in range(subgames):
            at = player * subgames + subgame
            by_line = by_line + jnp.where(row == line_ref[subgame], root[at : at + 1, :], 0.0)
        mine_lines = lines_in.at[flop]
        mine_lines[player * 8 : player * 8 + 8, :] = by_line
    for step in flop_steps:
        sent.append(
            remote(
                lines_in.at[flop], lines_in.at[flop], send_line.at[step], recv_line.at[flop], flop_peer(step)
            )
        )
        sent[-1].start()
    for step in flop_steps:
        peer = flop_peer(step)
        remote(
            lines_in.at[flop], lines_in.at[peer[0]], send_line.at[step], recv_line.at[peer[0]], peer
        ).wait_recv()
    total = lines_in[0]
    for number in range(1, flops):
        total = total + lines_in[number]
    total = total * scale
    for player in range(2):
        line_values = total[player * 8 : player * 8 + lines, :share]
        node = jnp.sum(own[player] * line_values, axis=0, keepdims=True)
        trunk_out[:, player] = jnp.maximum(trunk_ref[:, player] + line_values - node, 0.0)
    out_copy.wait()
    for copy in sent:
        copy.wait_send()


def on_device(flops, turns, trunk_regret, river_regret, line_pot, subgame_line, alive, ranks):
    subgames, turn_local, rivers, _, _, slots = river_regret.shape
    lines = trunk_regret.shape[1]
    scale = lines / (subgames * flops * turn_local * turns * rivers)
    packed = -(-((CARDS - 4) * (CARDS - 5) // 2) // LANES) * LANES
    compat = jnp.asarray(compat_table(packed, CARDS - 4).astype(jnp.bfloat16))
    cards = jnp.asarray(card_table(packed, CARDS - 4).astype(jnp.bfloat16))
    card_slots = jnp.asarray(card_table(packed, CARDS - 4).T.astype(jnp.bfloat16))
    ones = jnp.asarray(np.triu(np.ones((LANES, LANES)), 1).astype(jnp.bfloat16))
    by_line = trunk_regret.transpose(1, 0, 2)
    vmem = pl.BlockSpec(memory_space=pltpu.VMEM)
    hbm = pl.BlockSpec(memory_space=pl.ANY)
    boards = subgames * rivers
    tiles, packed_tiles = slots // LANES, packed // LANES
    rows = lambda count, tile_count=tiles: pltpu.VMEM((tile_count, count, LANES), F32)
    dma = lambda *shape: pltpu.SemaphoreType.DMA(shape)
    new_trunk, new_river = pl.pallas_call(
        functools.partial(iteration_kernel, flops, turns, scale),
        out_shape=(
            jax.ShapeDtypeStruct(by_line.shape, F32),
            jax.ShapeDtypeStruct(river_regret.shape, F32),
        ),
        in_specs=[hbm] * 10,
        out_specs=(vmem, hbm),
        scratch_shapes=[
            pltpu.SMEM(subgame_line.shape, jnp.int32),
            pltpu.SMEM(line_pot.shape, F32),
            pltpu.VMEM(by_line.shape, F32),
            pltpu.VMEM(river_regret.shape, F32),
            pltpu.VMEM(alive.shape, jnp.int32),
            pltpu.VMEM(ranks.shape, jnp.int32),
            pltpu.VMEM(compat.shape, BF16),
            pltpu.VMEM(cards.shape, BF16),
            pltpu.VMEM(card_slots.shape, BF16),
            pltpu.VMEM(ones.shape, BF16),
            rows(4 * boards),
            rows(4 * boards, packed_tiles),
            rows(2 * boards, packed_tiles),
            pltpu.VMEM((packed_tiles, 8, LANES), jnp.int32),
            pltpu.VMEM((tiles, 8, LANES), jnp.int32),
            rows(8),
            rows(boards, packed_tiles),
            rows(8, packed_tiles),
            pltpu.VMEM((READY, packed_tiles, packed, LANES), F8),
            rows(8 * boards, packed_tiles),
            rows(8 * boards, packed_tiles),
            rows(boards, packed_tiles),
            pltpu.VMEM((READY, 16, packed), BF16),
            pltpu.VMEM((READY, packed, LANES), BF16),
            pltpu.VMEM((16, slots), F32),
            pltpu.VMEM((16, LANES), F32),
            rows(16, turns),
            rows(8, turns),
            rows(8, turns),
            rows(8, packed_tiles),
            rows(16, flops),
            dma(10),
            pltpu.SemaphoreType.DMA,
            dma(turns),
            dma(turns),
            dma(turns),
            dma(turns),
            dma(flops),
            dma(flops),
        ],
        compiler_params=pltpu.CompilerParams(
            collective_id=0, has_side_effects=True, vmem_limit_bytes=60 * 2**20
        ),
        name="cfr_iteration",
    )(subgame_line, line_pot, by_line, river_regret, alive, ranks, compat, cards, card_slots, ones)
    return (new_trunk.transpose(1, 0, 2), new_river)


def solution(mesh):
    return jax.shard_map(
        functools.partial(on_device, mesh.shape["flop"], mesh.shape["turn"]),
        mesh=mesh,
        in_specs=(
            P(None, None, "turn"),
            P("flop", "turn", None, None, None, None),
            P(),
            P("flop"),
            P("flop", "turn", None, None),
            P("flop", "turn", None, None),
        ),
        out_specs=(P(None, None, "turn"), P("flop", "turn", None, None, None, None)),
        check_vma=False,
    )
```
